512 devices in a mesh: blk: 16 (over y, z_hi, core), act: 32 (over x, z_lo).
Axes of the slice: x: 4, y: 4, z: 16 (z_hi: 2, z_lo: 8; z = z_hi * 8 + z_lo), core: 2. Of those that a mesh axis runs over, the one named last changes fastest.
Arguments:
- star_state: float32 [12, 131072], P(None, 'blk'), may hold values from -4 to 4
- star_mass: float32 [131072], P('blk'), may hold values from 0.1 to 10
- star_level: int32 [131072], P('blk'), may hold values from 0 to 3, as said below
- active_slots: int32 [32768], P('act'), may hold values from -1 to 131071, as said below
Outputs:
- advanced: float32 [12, 32768], P(None, 'act')
The draws below stay inside these ranges and needn't reach their ends.
Inputs may be any that keep to these rules, and one draw needn't show every extreme that they name: `active_slots`: the indices of the level-2 stars, then -1 up to the next multiple of 128 slots, then the indices of the level-3 stars, then -1 to the end. Each of the two lists holds one star or more, both together exactly 13312; every star of level 2 or 3 appears once and no other star appears. `star_level`: exactly 13312 stars have level 2 or 3: those listed in active_slots.
All inputs are finite; a program needn't handle non-finite values.
Results may differ from the reference program's by a relative error of at most 0.0003.
Values sent between devices are 32-bit elements; how exact they have to be, the bound alone decides.
No kernel may reach another device: no remote copies, remote signals or barrier semaphores. Data moves between devices by JAX's collectives and lax.ppermute only.
A program may use at most 64 MiB of HBM per device.

```python
import math
import jax
import jax.numpy as jnp
from jax import lax

BLOCK = 128
STARS = 131072
SLOTS = 32768
ACTIVE = 13312


def joint_draw(key):
    ordering = jax.random.permutation(jax.random.fold_in(key, 11), STARS)
    first_count = jax.random.randint(jax.random.fold_in(key, 12), (), 1, ACTIVE)
    ranking = jnp.arange(STARS)
    slow_level = jax.random.randint(jax.random.fold_in(key, 13), (STARS,), 0, 2)
    rank_level = jnp.where(ranking < first_count, 2, jnp.where(ranking < ACTIVE, 3, slow_level)).astype(jnp.int32)
    levels = jnp.zeros((STARS,), jnp.int32).at[ordering].set(rank_level)
    padded = (first_count + BLOCK - 1) // BLOCK * BLOCK
    slot_position = jnp.arange(SLOTS)
    in_first = slot_position < first_count
    in_second = (slot_position >= padded) & (slot_position < padded + ACTIVE - first_count)
    second_rank = slot_position - padded + first_count
    source_rank = jnp.clip(jnp.where(in_first, slot_position, jnp.where(in_second, second_rank, 0)), 0, STARS - 1)
    listed = jnp.where(in_first | in_second, ordering[source_rank], -1).astype(jnp.int32)
    return (levels, listed)


def draw_star_level(key, part):
    return joint_draw(key)[0]


def draw_active_slots(key, part):
    return joint_draw(key)[1]


def block_levels(rng, shape, pieces, smallest, high):
    factor_of, own = 1.0, jax.random.fold_in(rng, 6)
    for dim, blocks in pieces:
        draws = jnp.exp(jax.random.uniform(jax.random.fold_in(own, dim), (blocks,), jnp.float32, smallest / len(pieces), high / len(pieces)))
        factor_of = factor_of * jnp.repeat(draws, shape[dim] // blocks).reshape([-1 if axis == dim else 1 for axis in range(len(shape))])
    return factor_of


def bell_draw(stream_key, shape, deviation, bound, shards=(), held_as=jnp.bfloat16):
    entries = deviation * jax.random.normal(stream_key, shape, jnp.float32)
    if shards:
        entries = entries * block_levels(stream_key, shape, shards, -0.22, 0.18)
    return jnp.clip(entries, -bound, bound).astype(held_as)


def setup_inputs(seed: int = 0) -> dict:
    arg_keys = jax.random.split(jax.random.key(seed), 5)
    return {
        "star_state": bell_draw(arg_keys[0], (12, STARS), 0.7, 4.0, ((1, 16),), jnp.float32),
        "star_mass": jnp.clip(jnp.exp(math.log(10.0) - 4.6051702 * jax.random.uniform(arg_keys[1], (STARS,), jnp.float32) ** block_levels(arg_keys[1], (STARS,), ((0, 16),), -0.2, 0.2)), 0.1, 10.0),
        "star_level": draw_star_level(jax.random.fold_in(arg_keys[4], 71), 0),
        "active_slots": draw_active_slots(jax.random.fold_in(arg_keys[4], 71), 0),
    }


SOFTENING = 0.0025
ONE_THIRD = 1.0 / 3.0
ONE_TWELFTH = 1.0 / 12.0

def since_update(level_value):
    return jnp.where(level_value == 0, 0.375, jnp.where(level_value == 1, 0.125, jnp.where(level_value == 2, 0.125, 0.0625))).astype(jnp.float32)

def predict(star_rows, elapsed_time):
    position = star_rows[0:3]
    velocity = star_rows[3:6]
    accel_old = star_rows[6:9]
    jerk_old = star_rows[9:12]
    new_place = position + elapsed_time * (velocity + elapsed_time * 0.5 * (accel_old + elapsed_time * ONE_THIRD * jerk_old))
    new_speed = velocity + elapsed_time * (accel_old + elapsed_time * 0.5 * jerk_old)
    return jnp.concatenate([new_place, new_speed], 0)

def pair_block(targets, sources, weights):
    offset = sources[0:3, None, :] - targets[0:3, :, None]
    relative = sources[3:6, None, :] - targets[3:6, :, None]
    radius_sq = lax.optimization_barrier(jnp.sum(offset * offset, 0)) + SOFTENING
    inverse = 1.0 / jnp.sqrt(radius_sq)
    inverse_sq = inverse * inverse
    strength = weights[None, :] * inverse * inverse_sq
    approach = lax.optimization_barrier(jnp.sum(offset * relative, 0)) * inverse_sq
    new_accel = lax.optimization_barrier(jnp.sum(strength * offset, 2))
    new_jerk = lax.optimization_barrier(jnp.sum(strength * (relative - 3.0 * approach * offset), 2))
    return jnp.concatenate([new_accel, new_jerk], 0)

def pair_sum(targets, sources, weights):
    source_count = sources.shape[1]
    block_size = math.gcd(source_count, 1024)
    block_count = source_count // block_size

    def add_part(turn, running):
        first_index = (turn * block_size).astype(jnp.int32)
        source_part = lax.dynamic_slice_in_dim(sources, first_index, block_size, 1)
        weight_part = lax.dynamic_slice_in_dim(weights, first_index, block_size, 0)
        return running + pair_block(targets, source_part, weight_part)
    return lax.fori_loop(0, block_count, add_part, jnp.zeros((6, targets.shape[1]), jnp.float32))

def correct(previous, forces, elapsed_time):
    position = previous[0:3]
    velocity = previous[3:6]
    accel_old = previous[6:9]
    jerk_old = previous[9:12]
    new_accel = forces[0:3]
    new_jerk = forces[3:6]
    half_step = 0.5 * elapsed_time
    step_sq = elapsed_time * elapsed_time * ONE_TWELFTH
    new_velocity = velocity + half_step * (accel_old + new_accel) + step_sq * (jerk_old - new_jerk)
    new_position = position + half_step * (velocity + new_velocity) + step_sq * (accel_old - new_accel)
    return jnp.concatenate([new_position, new_velocity, new_accel, new_jerk], 0)

def reference(star_state, star_mass, star_level, active_slots):
    elapsed_time = since_update(star_level)
    predicted = predict(star_state, elapsed_time)
    weights = star_mass / STARS
    live_slots = active_slots >= 0
    slot_index = jnp.maximum(active_slots, 0).astype(jnp.int32)
    previous = jnp.take(star_state, slot_index, axis=1)
    slot_elapsed = jnp.take(elapsed_time, slot_index)
    targets = predict(previous, slot_elapsed)
    block_total = SLOTS // BLOCK
    target_blocks = targets.reshape(6, block_total, BLOCK).transpose(1, 0, 2)
    live_blocks = live_slots.reshape(block_total, BLOCK)

    def block_force(block_args):
        block_rows, block_live = block_args
        return lax.cond(jnp.any(block_live), lambda: pair_sum(block_rows, predicted, weights), lambda: jnp.zeros((6, BLOCK), jnp.float32))
    forces = lax.map(block_force, (target_blocks, live_blocks))
    forces = forces.transpose(1, 0, 2).reshape(6, SLOTS)
    result = correct(previous, forces, slot_elapsed)
    return jnp.where(live_slots[None, :], result, 0.0)
```

```python
import functools

import jax
import jax.numpy as jnp
from jax import lax
from jax.experimental import pallas as pl
from jax.experimental.pallas import tpu as pltpu
from jax.sharding import Mesh, PartitionSpec as P

SOFTENING = 0.0025
STARS = 131072
ONE_THIRD = 1.0 / 3.0
ONE_TWELFTH = 1.0 / 12.0
bf16 = jnp.bfloat16
f32 = jnp.float32
AXES = ("y", "zh", "core", "xh", "xl", "zl")
SIZES = (4, 2, 2, 2, 2, 8)
BLK = ("y", "zh", "core")
ACT = ("xh", "xl", "zl")
SHARD = 8192
HALF = 512
PART = 256
MEMBERS = 16
CHUNK = 512
SOURCES = 2 * SHARD
FULL = pl.BlockSpec(memory_space=pltpu.VMEM)
SCALARS = pl.BlockSpec(memory_space=pltpu.SMEM)
PARAMS = pltpu.CompilerParams(vmem_limit_bytes=48 * 2**20)
NN = (((1,), (0,)), ((), ()))
TN = (((0,), (0,)), ((), ()))
dot = functools.partial(lax.dot_general, preferred_element_type=f32)


def exchange_groups():
    groups = []
    for core in range(2):
        for x in range(2):
            for zl in range(8):
                groups.append(
                    [
                        (((y * 2 + zh) * 2 + core) * 4 + column) * 8 + zl
                        for y in range(4)
                        for zh in range(2)
                        for column in (x, 3 - x)
                    ]
                )
    return groups


def rows_of(value):
    return lax.broadcasted_iota(jnp.int32, value.shape, 0)


def split(value):
    high = value.astype(bf16).astype(f32)
    rest = value - high
    middle = rest.astype(bf16).astype(f32)
    return high, middle, rest - middle


def high_low(value):
    high = value.astype(bf16)
    return high, (value - high.astype(f32)).astype(bf16)


def table_kernel(state, mass, level, table):
    lev = level[...]
    dt = jnp.where(lev == 0, 0.375, jnp.where(lev == 3, 0.0625, 0.125)).astype(f32)
    x, v, a, j = state[0:3], state[3:6], state[6:9], state[9:12]
    place = x + dt * (v + dt * 0.5 * (a + dt * ONE_THIRD * j))
    speed = v + dt * (a + dt * 0.5 * j)
    step_sq = dt * dt * ONE_TWELFTH
    half = 0.5 * dt
    table[0:3, :] = place
    table[3:6, :] = speed
    table[6:7, :] = mass[...]
    table[7:8, :] = dt
    table[8:11, :] = x + half * v + step_sq * a
    table[11:14, :] = v + half * a + step_sq * j
    table[14:15, :] = jnp.sum(place * place, 0, keepdims=True)
    table[15:16, :] = 3.0 * jnp.sum(place * speed, 0, keepdims=True)


def lookup_kernel(where, slots, mine, other, out):
    first, core = where[0], where[1]
    tables = ((mine, first + core * SHARD), (other, first + (1 - core) * SHARD))
    groups = HALF // 128
    index = slots[pl.ds(core * groups, groups), :]
    picked = [(jnp.zeros((8, 128), f32),) * 2 for _ in range(groups)]
    for table, start in tables:
        local_index = index - start
        low = [jnp.broadcast_to((local_index & 127)[g : g + 1], (8, 128)) for g in range(groups)]
        high = [jnp.broadcast_to((local_index >> 7)[g : g + 1], (8, 128)) for g in range(groups)]

        def look(h, carry):
            at = pl.ds(pl.multiple_of(h * 128, 128), 128)
            tiles = (table[0:8, at], table[8:16, at])
            result = []
            for g in range(groups):
                hit = high[g] == h
                result.append(
                    tuple(
                        jnp.where(
                            hit,
                            jnp.take_along_axis(
                                tiles[k], low[g], axis=1, mode="promise_in_bounds"
                            ),
                            carry[g][k],
                        )
                        for k in range(2)
                    )
                )
            return result

        picked = lax.fori_loop(0, SHARD // 128, look, picked, unroll=4)
    for member in range(MEMBERS):
        for part in range(2):
            g = (member % 2) * 2 + part
            for k in range(2):
                out[member, 8 * k : 8 * k + 8, part * 128 : (part + 1) * 128] = picked[g][k]


def source_features(table, features, pull, swing, offset):
    def step(turn, _):
        at = pl.ds(pl.multiple_of(turn * CHUNK, CHUNK), CHUNK)
        to = pl.ds(pl.multiple_of(offset + turn * CHUNK, CHUNK), CHUNK)
        upper, lower = table[0:8, at], table[8:16, at]
        row = rows_of(upper)
        a, b, c = split(jnp.where(row == 7, 1.0, upper))
        d, e, f = split(lower)
        zero = jnp.zeros_like(a)
        pairs = ((a, a), (a, b), (b, c), (d, e), (f, zero))
        for k, pair in enumerate(pairs):
            features[16 * k : 16 * k + 16, to] = jnp.concatenate(pair, 0).astype(bf16)
        weight = upper[6:7] * (1.0 / STARS)
        moved = jnp.where(row == 7, 0.0, jnp.where(row == 6, 1.0, upper)) * weight
        placed = pltpu.roll(moved, 3, 0)
        turned = jnp.where(row == 7, weight, jnp.where((row >= 3) & (row < 6), -placed, 0.0))
        for ref, value in ((pull, moved), (swing, turned)):
            a, b, c = split(value)
            ref[0:16, to] = jnp.concatenate((a, b), 0).astype(bf16)
            ref[16:32, to] = jnp.concatenate((c, zero), 0).astype(bf16)
        return 0

    lax.fori_loop(0, SHARD // CHUNK, step, 0)


def target_features(target):
    row = rows_of(target)
    place = jnp.where(row < 3, target, 0.0)
    speed = pltpu.roll(target, 5, 0)
    place_sq = jnp.sum(place * place, 0, keepdims=True) + SOFTENING
    product = 3.0 * jnp.sum(place * speed, 0, keepdims=True)
    shifted = pltpu.roll(target, 3, 0)
    radius = jnp.where(row == 7, place_sq, -2.0 * place)
    near = jnp.where(
        row == 7,
        product,
        jnp.where(row < 3, -3.0 * speed, jnp.where(row < 6, -3.0 * shifted, 0.0)),
    )
    zero = jnp.zeros_like(target)
    result = []
    for value, own_row in ((radius, 6), (near, 7)):
        a, b, c = split(value)
        one = jnp.where(row == own_row, 1.0, 0.0)
        result.append(
            jnp.concatenate((a, b, c, a, b, a, one, one, one, zero), 0).astype(bf16)
        )
    return result


def force_kernel(received, mine, other, out, features, pull, swing, total):
    target_rows = received[0]
    for sender in range(2, MEMBERS, 2):
        target_rows = target_rows + received[sender]
    target = target_rows[0:8]
    source_features(mine, features, pull, swing, 0)
    source_features(other, features, pull, swing, SHARD)
    radius_part, near_part = target_features(target)
    total[...] = jnp.zeros_like(total)

    def step(turn, _):
        at = pl.ds(pl.multiple_of(turn * CHUNK, CHUNK), CHUNK)
        source = features[:, at]
        radius_sq = dot(source, radius_part, TN)
        product = dot(source, near_part, TN)
        inverse = lax.rsqrt(radius_sq)
        inverse_sq = inverse * inverse
        strength = inverse_sq * inverse
        turning = (product * inverse_sq) * strength
        pulls, swings = pull[:, at], swing[:, at]
        total[...] += dot(
            jnp.concatenate((pulls, pulls, swings, swings), 1),
            jnp.concatenate(high_low(strength) + high_low(turning), 0),
            NN,
        )
        return 0

    lax.fori_loop(0, SOURCES // CHUNK, step, 0, unroll=2)
    sums = total[0:8] + total[8:16] + total[16:24]
    place, speed = target[0:3], target[3:6]
    accel = sums[0:3] - place * sums[6:7]
    jerk = sums[3:6] - speed * sums[6:7] + place * sums[7:8]
    for member in range(MEMBERS):
        out[member, 0:3, :] = accel
        out[member, 3:6, :] = jerk
        out[member, 6:8, :] = target[6:8]
        out[member, 8:16, :] = target_rows[8:16]


def correct_kernel(received, out):
    for part in range(2):
        rows = received[part]
        force = rows[0:8]
        for sender in range(part + 2, MEMBERS, 2):
            force = force + received[sender, 0:8, :]
        dt = rows[7:8]
        accel, jerk = force[0:3], force[3:6]
        half = 0.5 * dt
        step_sq = dt * dt * ONE_TWELFTH
        velocity = rows[11:14] + half * accel - step_sq * jerk
        base = rows[8:11]
        position = base + half * velocity - step_sq * accel
        at = slice(part * PART, (part + 1) * PART)
        out[0:3, at] = position
        out[3:6, at] = velocity
        out[6:9, at] = accel
        out[9:12, at] = jerk


def local(star_state, star_mass, star_level, active_slots):
    core = lax.axis_index("core")
    pair = lax.axis_index("y") * 2 + lax.axis_index("zh")
    where = jnp.stack([pair * SOURCES, core]).astype(jnp.int32)
    table = pl.pallas_call(
        table_kernel,
        out_shape=jax.ShapeDtypeStruct((16, SHARD), f32),
        in_specs=[FULL] * 3,
        out_specs=FULL,
        compiler_params=PARAMS,
        name="table",
    )(star_state, star_mass.reshape(1, SHARD), star_level.reshape(1, SHARD))
    other = lax.ppermute(table, "core", [(0, 1), (1, 0)])
    groups = exchange_groups()
    sent = pl.pallas_call(
        lookup_kernel,
        out_shape=jax.ShapeDtypeStruct((MEMBERS, 16, PART), f32),
        in_specs=[SCALARS] + [FULL] * 3,
        out_specs=FULL,
        compiler_params=PARAMS,
        name="lookup",
    )(where, active_slots.reshape(8, 128), table, other)
    received = lax.all_to_all(sent, AXES, 0, 0, axis_index_groups=groups)
    partial = pl.pallas_call(
        force_kernel,
        out_shape=jax.ShapeDtypeStruct((MEMBERS, 16, PART), f32),
        in_specs=[FULL] * 3,
        out_specs=FULL,
        scratch_shapes=[
            pltpu.VMEM((80, SOURCES), bf16),
            pltpu.VMEM((32, SOURCES), bf16),
            pltpu.VMEM((32, SOURCES), bf16),
            pltpu.VMEM((32, PART), f32),
        ],
        compiler_params=PARAMS,
        name="forces",
    )(received, table, other)
    shares = lax.all_to_all(partial, AXES, 0, 0, axis_index_groups=groups)
    half_result = pl.pallas_call(
        correct_kernel,
        out_shape=jax.ShapeDtypeStruct((12, HALF), f32),
        in_specs=[FULL],
        out_specs=FULL,
        compiler_params=PARAMS,
        name="corrector",
    )(shares)
    halves = lax.all_gather(half_result, "core")
    result = jnp.concatenate([halves[0], halves[1]], 1)
    return jnp.where((active_slots >= 0)[None, :], result, 0.0)


def solution(mesh):
    split_mesh = Mesh(mesh.devices.reshape(SIZES), AXES)
    return jax.shard_map(
        local,
        mesh=split_mesh,
        in_specs=(P(None, BLK), P(BLK), P(BLK), P(ACT)),
        out_specs=P(None, ACT),
        check_vma=False,
    )
```

```python
import functools

import jax
import jax.numpy as jnp
from jax import lax
from jax.experimental import pallas as pl
from jax.experimental.pallas import tpu as pltpu
from jax.sharding import Mesh, PartitionSpec as P

SOFTENING = 0.0025
STARS = 131072
ONE_THIRD = 1.0 / 3.0
ONE_TWELFTH = 1.0 / 12.0
bf16 = jnp.bfloat16
f32 = jnp.float32
AXES = ("y", "zh", "core", "xh", "xl", "zl")
SIZES = (4, 2, 2, 2, 2, 8)
BLK = ("y", "zh", "core")
ACT = ("xh", "xl", "zl")
SHARD = 8192
HALF = 512
PART = 256
SENDERS = 8
MEMBERS = 16
CHUNK = 512
SOURCES = 2 * SHARD
FULL = pl.BlockSpec(memory_space=pltpu.VMEM)
SCALARS = pl.BlockSpec(memory_space=pltpu.SMEM)
PARAMS = pltpu.CompilerParams(vmem_limit_bytes=48 * 2**20)
NN = (((1,), (0,)), ((), ()))
TN = (((0,), (0,)), ((), ()))
dot = functools.partial(lax.dot_general, preferred_element_type=f32)


def exchange_groups():
    groups = []
    for core in range(2):
        for x in range(2):
            for zl in range(8):
                groups.append(
                    [
                        (((y * 2 + zh) * 2 + core) * 4 + column) * 8 + zl
                        for y in range(4)
                        for zh in range(2)
                        for column in (x, 3 - x)
                    ]
                )
    return groups


def rows_of(value):
    return lax.broadcasted_iota(jnp.int32, value.shape, 0)


def split(value):
    high = value.astype(bf16).astype(f32)
    rest = value - high
    middle = rest.astype(bf16).astype(f32)
    return high, middle, rest - middle


def high_low(value):
    high = value.astype(bf16)
    return high, (value - high.astype(f32)).astype(bf16)


def table_kernel(state_in, mass_in, level_in, table, state, mass, level, done):
    copies = [
        pltpu.make_async_copy(source, target, done.at[k])
        for k, (source, target) in enumerate(
            ((state_in, state), (mass_in, mass), (level_in, level))
        )
    ]
    for copy in copies:
        copy.start()
    for copy in copies:
        copy.wait()
    lev = level[...]
    dt = jnp.where(lev == 0, 0.375, jnp.where(lev == 3, 0.0625, 0.125)).astype(f32)
    x, v, a, j = state[0:3], state[3:6], state[6:9], state[9:12]
    place = x + dt * (v + dt * 0.5 * (a + dt * ONE_THIRD * j))
    speed = v + dt * (a + dt * 0.5 * j)
    step_sq = dt * dt * ONE_TWELFTH
    half = 0.5 * dt
    table[0:3, :] = place
    table[3:6, :] = speed
    table[6:7, :] = mass[...]
    table[7:8, :] = dt
    table[8:11, :] = x + half * v + step_sq * a
    table[11:14, :] = v + half * a + step_sq * j
    table[14:15, :] = jnp.sum(place * place, 0, keepdims=True)
    table[15:16, :] = 3.0 * jnp.sum(place * speed, 0, keepdims=True)


def lookup_kernel(where, own_slots, passed_slots, mine, other, out):
    first, core, helper = where[0], where[1], where[2]
    at = pl.ds(core * 4 + helper * 2, 2)
    index = jnp.where(helper == 0, own_slots[at, :], passed_slots[at, :])
    index = jnp.concatenate((index[0:1], index[1:2]), 1)
    picked = jnp.zeros((16, PART), f32)
    for table, start in ((mine, first + core * SHARD), (other, first + (1 - core) * SHARD)):
        local_index = index - start
        low, high = local_index & 127, local_index >> 7
        low = jnp.broadcast_to(low, (128, PART))
        hit = jnp.where(rows_of(low) == low, 1.0, 0.0).astype(bf16)
        hits = jnp.concatenate((hit, hit, hit), 0)
        high = jnp.broadcast_to(high, (16, PART))
        for block in range(SHARD // 2048):
            tiles = [
                table[:, (block * 16 + i) * 128 : (block * 16 + i + 1) * 128] for i in range(16)
            ]
            parts = [part.astype(bf16) for part in split(jnp.concatenate(tiles, 0))]
            found = dot(jnp.concatenate(parts, 1), hits, NN)
            for i in range(16):
                picked = jnp.where(high == block * 16 + i, found[16 * i : 16 * i + 16], picked)
    for member in range(SENDERS):
        out[member] = picked


def source_features(table, features, pull, swing, offset):
    def step(turn, _):
        at = pl.ds(pl.multiple_of(turn * CHUNK, CHUNK), CHUNK)
        to = pl.ds(pl.multiple_of(offset + turn * CHUNK, CHUNK), CHUNK)
        upper, lower = table[0:8, at], table[8:16, at]
        row = rows_of(upper)
        a, b, c = split(jnp.where(row == 7, 1.0, upper))
        d, e, f = split(lower)
        zero = jnp.zeros_like(a)
        pairs = ((a, a), (a, b), (b, c), (d, e), (f, zero))
        for k, pair in enumerate(pairs):
            features[16 * k : 16 * k + 16, to] = jnp.concatenate(pair, 0).astype(bf16)
        weight = upper[6:7] * (1.0 / STARS)
        moved = jnp.where(row == 7, 0.0, jnp.where(row == 6, 1.0, upper)) * weight
        placed = pltpu.roll(moved, 3, 0)
        turned = jnp.where(row == 7, weight, jnp.where((row >= 3) & (row < 6), -placed, 0.0))
        for ref, value in ((pull, moved), (swing, turned)):
            a, b, c = split(value)
            ref[0:16, to] = jnp.concatenate((a, b), 0).astype(bf16)
            ref[16:32, to] = jnp.concatenate((c, zero), 0).astype(bf16)
        return 0

    lax.fori_loop(0, SHARD // CHUNK, step, 0)


def target_features(target):
    row = rows_of(target)
    place = jnp.where(row < 3, target, 0.0)
    speed = pltpu.roll(target, 5, 0)
    place_sq = jnp.sum(place * place, 0, keepdims=True) + SOFTENING
    product = 3.0 * jnp.sum(place * speed, 0, keepdims=True)
    shifted = pltpu.roll(target, 3, 0)
    radius = jnp.where(row == 7, place_sq, -2.0 * place)
    near = jnp.where(
        row == 7,
        product,
        jnp.where(row < 3, -3.0 * speed, jnp.where(row < 6, -3.0 * shifted, 0.0)),
    )
    zero = jnp.zeros_like(target)
    result = []
    for value, own_row in ((radius, 6), (near, 7)):
        a, b, c = split(value)
        one = jnp.where(row == own_row, 1.0, 0.0)
        result.append(
            jnp.concatenate((a, b, c, a, b, a, one, one, one, zero), 0).astype(bf16)
        )
    return result


def force_kernel(where, received, mine, other, out, features, pull, swing, total, rows):
    target_rows = received[0]
    for sender in range(1, SENDERS):
        target_rows = target_rows + received[sender]
    target = target_rows[0:8]
    rows[...] = target_rows
    source_features(mine, features, pull, swing, 0)
    source_features(other, features, pull, swing, SHARD)
    radius_part, near_part = target_features(target)
    total[...] = jnp.zeros_like(total)

    def step(turn, _):
        at = pl.ds(pl.multiple_of(turn * CHUNK, CHUNK), CHUNK)
        source = features[:, at]
        radius_sq = dot(source, radius_part, TN)
        product = dot(source, near_part, TN)
        inverse = lax.rsqrt(radius_sq)
        inverse_sq = inverse * inverse
        strength = inverse_sq * inverse
        turning = (product * inverse_sq) * strength
        pulls, swings = pull[:, at], swing[:, at]
        total[...] += dot(
            jnp.concatenate((pulls, pulls, swings, swings), 1),
            jnp.concatenate(high_low(strength) + high_low(turning), 0),
            NN,
        )
        return 0

    lax.fori_loop(0, SOURCES // CHUNK, step, 0, unroll=2)
    sums = total[0:8] + total[8:16] + total[16:24]
    place, speed = target[0:3], target[3:6]
    accel = sums[0:3] - place * sums[6:7]
    jerk = sums[3:6] - speed * sums[6:7] + place * sums[7:8]
    spare = rows[pl.ds(7 + where[3], 1), :]
    for member in range(MEMBERS):
        out[member, 0:3, :] = accel
        out[member, 3:6, :] = jerk
        out[member, 6:7, :] = spare
        out[member, 7:8, :] = spare


def correct_kernel(received, out):
    for part in range(2):
        force = received[part]
        for sender in range(1, SENDERS):
            force = force + received[2 * sender + part]
        dt = received[part, 6:7, :]
        bases = [received[2 * sender + part, 6:7, :] for sender in range(1, 7)]
        accel, jerk = force[0:3], force[3:6]
        half = 0.5 * dt
        step_sq = dt * dt * ONE_TWELFTH
        velocity = jnp.concatenate(bases[3:6], 0) + half * accel - step_sq * jerk
        position = jnp.concatenate(bases[0:3], 0) + half * velocity - step_sq * accel
        at = slice(part * PART, (part + 1) * PART)
        out[0:3, at] = position
        out[3:6, at] = velocity
        out[6:9, at] = accel
        out[9:12, at] = jerk


def local(star_state, star_mass, star_level, active_slots):
    core, helper = lax.axis_index("core"), lax.axis_index("xh")
    sender = lax.axis_index("y") * 2 + lax.axis_index("zh")
    where = jnp.stack([sender * SOURCES, core, helper, sender]).astype(jnp.int32)
    slots = active_slots.reshape(8, 128)
    passed = lax.ppermute(slots, ("xh", "xl"), [(x, 3 - x) for x in range(4)])
    anywhere = pl.BlockSpec(memory_space=pl.ANY)
    table = pl.pallas_call(
        table_kernel,
        out_shape=jax.ShapeDtypeStruct((16, SHARD), f32),
        in_specs=[anywhere] * 3,
        out_specs=FULL,
        scratch_shapes=[
            pltpu.VMEM((12, SHARD), f32),
            pltpu.VMEM((1, SHARD), f32),
            pltpu.VMEM((1, SHARD), jnp.int32),
            pltpu.SemaphoreType.DMA((3,)),
        ],
        compiler_params=PARAMS,
        name="table",
    )(star_state, star_mass.reshape(1, SHARD), star_level.reshape(1, SHARD))
    other = lax.ppermute(table, "core", [(0, 1), (1, 0)])
    sent = pl.pallas_call(
        lookup_kernel,
        out_shape=jax.ShapeDtypeStruct((SENDERS, 16, PART), f32),
        in_specs=[SCALARS] + [FULL] * 4,
        out_specs=FULL,
        compiler_params=PARAMS,
        name="lookup",
    )(where, slots, passed, table, other)
    received = lax.all_to_all(sent, ("y", "zh"), 0, 0)
    partial = pl.pallas_call(
        force_kernel,
        out_shape=jax.ShapeDtypeStruct((MEMBERS, 8, PART), f32),
        in_specs=[SCALARS] + [FULL] * 3,
        out_specs=FULL,
        scratch_shapes=[
            pltpu.VMEM((80, SOURCES), bf16),
            pltpu.VMEM((32, SOURCES), bf16),
            pltpu.VMEM((32, SOURCES), bf16),
            pltpu.VMEM((32, PART), f32),
            pltpu.VMEM((16, PART), f32),
        ],
        compiler_params=PARAMS,
        name="forces",
    )(where, received, table, other)
    shares = lax.all_to_all(partial, AXES, 0, 0, axis_index_groups=exchange_groups())
    half_result = pl.pallas_call(
        correct_kernel,
        out_shape=jax.ShapeDtypeStruct((12, HALF), f32),
        in_specs=[FULL],
        out_specs=FULL,
        compiler_params=PARAMS,
        name="corrector",
    )(shares)
    halves = lax.all_gather(half_result, "core")
    result = jnp.concatenate([halves[0], halves[1]], 1)
    return jnp.where((active_slots >= 0)[None, :], result, 0.0)


def solution(mesh):
    split_mesh = Mesh(mesh.devices.reshape(SIZES), AXES)
    return jax.shard_map(
        local,
        mesh=split_mesh,
        in_specs=(P(None, BLK), P(BLK), P(BLK), P(ACT)),
        out_specs=P(None, ACT),
        check_vma=False,
    )
```

```python
import functools

import jax
import jax.numpy as jnp
from jax import lax
from jax.experimental import pallas as pl
from jax.experimental.pallas import tpu as pltpu
from jax.sharding import Mesh, PartitionSpec as P

SOFTENING = 0.0025
STARS = 131072
ONE_THIRD = 1.0 / 3.0
ONE_TWELFTH = 1.0 / 12.0
bf16 = jnp.bfloat16
f32 = jnp.float32
AXES = ("y", "zh", "core", "xh", "xl", "zl")
SIZES = (4, 2, 2, 2, 2, 8)
BLK = ("y", "zh", "core")
ACT = ("xh", "xl", "zl")
SHARD = 8192
HALF = 512
PART = 256
SENDERS = 8
MEMBERS = 16
CHUNK = 512
SOURCES = 2 * SHARD
FULL = pl.BlockSpec(memory_space=pltpu.VMEM)
SCALARS = pl.BlockSpec(memory_space=pltpu.SMEM)
PARAMS = pltpu.CompilerParams(vmem_limit_bytes=48 * 2**20)
NN = (((1,), (0,)), ((), ()))
TN = (((0,), (0,)), ((), ()))
dot = functools.partial(lax.dot_general, preferred_element_type=f32)


def exchange_groups():
    groups = []
    for core in range(2):
        for x in range(2):
            for zl in range(8):
                groups.append(
                    [
                        (((y * 2 + zh) * 2 + core) * 4 + column) * 8 + zl
                        for y in range(4)
                        for zh in range(2)
                        for column in (x, 3 - x)
                    ]
                )
    return groups


def rows_of(value):
    return lax.broadcasted_iota(jnp.int32, value.shape, 0)


def split(value):
    high = value.astype(bf16).astype(f32)
    rest = value - high
    middle = rest.astype(bf16).astype(f32)
    return high, middle, rest - middle


def high_low(value):
    high = value.astype(bf16)
    return high, (value - high.astype(f32)).astype(bf16)


def table_kernel(state_in, mass_in, level_in, table, state, mass, level, done):
    copies = [
        pltpu.make_async_copy(source, target, done.at[k])
        for k, (source, target) in enumerate(
            ((state_in, state), (mass_in, mass), (level_in, level))
        )
    ]
    for copy in copies:
        copy.start()
    for copy in copies:
        copy.wait()
    lev = level[...]
    dt = jnp.where(lev == 0, 0.375, jnp.where(lev == 3, 0.0625, 0.125)).astype(f32)
    x, v, a, j = state[0:3], state[3:6], state[6:9], state[9:12]
    place = x + dt * (v + dt * 0.5 * (a + dt * ONE_THIRD * j))
    speed = v + dt * (a + dt * 0.5 * j)
    step_sq = dt * dt * ONE_TWELFTH
    half = 0.5 * dt
    table[0:3, :] = place
    table[3:6, :] = speed
    table[6:7, :] = mass[...]
    table[7:8, :] = dt
    table[8:11, :] = x + half * v + step_sq * a
    table[11:14, :] = v + half * a + step_sq * j
    table[14:15, :] = jnp.sum(place * place, 0, keepdims=True)
    table[15:16, :] = 3.0 * jnp.sum(place * speed, 0, keepdims=True)


def lookup_kernel(where, own_slots, passed_slots, mine, other, out):
    first, core, helper = where[0], where[1], where[2]
    at = pl.ds(core * 4 + helper * 2, 2)
    index = jnp.where(helper == 0, own_slots[at, :], passed_slots[at, :])
    index = jnp.concatenate((index[0:1], index[1:2]), 1)
    picked = jnp.zeros((16, PART), f32)
    for table, start in ((mine, first + core * SHARD), (other, first + (1 - core) * SHARD)):
        local_index = index - start
        low, high = local_index & 127, local_index >> 7
        low = jnp.broadcast_to(low, (128, PART))
        hit = jnp.where(rows_of(low) == low, 1.0, 0.0).astype(bf16)
        hits = jnp.concatenate((hit, hit, hit), 0)
        high = jnp.broadcast_to(high, (16, PART))
        for block in range(SHARD // 2048):
            tiles = [
                table[:, (block * 16 + i) * 128 : (block * 16 + i + 1) * 128] for i in range(16)
            ]
            parts = [part.astype(bf16) for part in split(jnp.concatenate(tiles, 0))]
            found = dot(jnp.concatenate(parts, 1), hits, NN)
            for i in range(16):
                picked = jnp.where(high == block * 16 + i, found[16 * i : 16 * i + 16], picked)
    for member in range(SENDERS):
        out[member] = picked


def source_features(table, features, pull, swing, offset):
    def step(turn, _):
        at = pl.ds(pl.multiple_of(turn * CHUNK, CHUNK), CHUNK)
        to = pl.ds(pl.multiple_of(offset + turn * CHUNK, CHUNK), CHUNK)
        upper, lower = table[0:8, at], table[8:16, at]
        row = rows_of(upper)
        a, b, c = split(jnp.where(row == 7, 1.0, upper))
        d, e, f = split(lower)
        zero = jnp.zeros_like(a)
        pairs = ((a, a), (a, b), (b, c), (d, e), (f, zero))
        for k, pair in enumerate(pairs):
            features[16 * k : 16 * k + 16, to] = jnp.concatenate(pair, 0).astype(bf16)
        weight = upper[6:7] * (1.0 / STARS)
        moved = jnp.where(row == 7, 0.0, jnp.where(row == 6, 1.0, upper)) * weight
        placed = pltpu.roll(moved, 3, 0)
        turned = jnp.where(row == 7, weight, jnp.where((row >= 3) & (row < 6), -placed, 0.0))
        for ref, value in ((pull, moved), (swing, turned)):
            a, b, c = split(value)
            ref[0:16, to] = jnp.concatenate((a, b), 0).astype(bf16)
            ref[16:32, to] = jnp.concatenate((c, zero), 0).astype(bf16)
        return 0

    lax.fori_loop(0, SHARD // CHUNK, step, 0)


def target_features(target):
    row = rows_of(target)
    place = jnp.where(row < 3, target, 0.0)
    speed = pltpu.roll(target, 5, 0)
    place_sq = jnp.sum(place * place, 0, keepdims=True) + SOFTENING
    product = 3.0 * jnp.sum(place * speed, 0, keepdims=True)
    shifted = pltpu.roll(target, 3, 0)
    radius = jnp.where(row == 7, place_sq, -2.0 * place)
    near = jnp.where(
        row == 7,
        product,
        jnp.where(row < 3, -3.0 * speed, jnp.where(row < 6, -3.0 * shifted, 0.0)),
    )
    zero = jnp.zeros_like(target)
    result = []
    for value, own_row in ((radius, 6), (near, 7)):
        a, b, c = split(value)
        one = jnp.where(row == own_row, 1.0, 0.0)
        result.append(
            jnp.concatenate((a, b, c, a, b, a, one, one, one, zero), 0).astype(bf16)
        )
    return result


def force_kernel(where, received, mine, other, out, features, pull, swing, total, rows):
    target_rows = received[0]
    for sender in range(1, SENDERS):
        target_rows = target_rows + received[sender]
    target = target_rows[0:8]
    rows[...] = target_rows
    source_features(mine, features, pull, swing, 0)
    source_features(other, features, pull, swing, SHARD)
    radius_part, near_part = target_features(target)
    total[...] = jnp.zeros_like(total)

    def step(turn, _):
        at = pl.ds(pl.multiple_of(turn * CHUNK, CHUNK), CHUNK)
        source = features[:, at]
        radius_sq = dot(source, radius_part, TN)
        product = dot(source, near_part, TN)
        inverse = lax.rsqrt(radius_sq)
        inverse_sq = inverse * inverse
        strength = inverse_sq * inverse
        turning = (product * inverse_sq) * strength
        pulls, swings = pull[:, at], swing[:, at]
        total[...] += dot(
            jnp.concatenate((pulls, pulls, swings, swings), 1),
            jnp.concatenate(high_low(strength) + high_low(turning), 0),
            NN,
        )
        return 0

    lax.fori_loop(0, SOURCES // CHUNK, step, 0, unroll=16)
    sums = total[0:8] + total[8:16] + total[16:24]
    place, speed = target[0:3], target[3:6]
    accel = sums[0:3] - place * sums[6:7]
    jerk = sums[3:6] - speed * sums[6:7] + place * sums[7:8]
    spare = rows[pl.ds(7 + where[3], 1), :]
    for member in range(MEMBERS):
        out[member, 0:3, :] = accel
        out[member, 3:6, :] = jerk
        out[member, 6:7, :] = spare
        out[member, 7:8, :] = spare


def correct_kernel(received, out):
    for part in range(2):
        force = received[part]
        for sender in range(1, SENDERS):
            force = force + received[2 * sender + part]
        dt = received[part, 6:7, :]
        bases = [received[2 * sender + part, 6:7, :] for sender in range(1, 7)]
        accel, jerk = force[0:3], force[3:6]
        half = 0.5 * dt
        step_sq = dt * dt * ONE_TWELFTH
        velocity = jnp.concatenate(bases[3:6], 0) + half * accel - step_sq * jerk
        position = jnp.concatenate(bases[0:3], 0) + half * velocity - step_sq * accel
        at = slice(part * PART, (part + 1) * PART)
        out[0:3, at] = position
        out[3:6, at] = velocity
        out[6:9, at] = accel
        out[9:12, at] = jerk


def local(star_state, star_mass, star_level, active_slots):
    core, helper = lax.axis_index("core"), lax.axis_index("xh")
    sender = lax.axis_index("y") * 2 + lax.axis_index("zh")
    where = jnp.stack([sender * SOURCES, core, helper, sender]).astype(jnp.int32)
    slots = active_slots.reshape(8, 128)
    passed = lax.ppermute(slots, ("xh", "xl"), [(x, 3 - x) for x in range(4)])
    anywhere = pl.BlockSpec(memory_space=pl.ANY)
    table = pl.pallas_call(
        table_kernel,
        out_shape=jax.ShapeDtypeStruct((16, SHARD), f32),
        in_specs=[anywhere] * 3,
        out_specs=FULL,
        scratch_shapes=[
            pltpu.VMEM((12, SHARD), f32),
            pltpu.VMEM((1, SHARD), f32),
            pltpu.VMEM((1, SHARD), jnp.int32),
            pltpu.SemaphoreType.DMA((3,)),
        ],
        compiler_params=PARAMS,
        cost_estimate=pl.CostEstimate(
            flops=10**10, bytes_accessed=120 * SHARD, transcendentals=0
        ),
        name="table",
    )(star_state, star_mass.reshape(1, SHARD), star_level.reshape(1, SHARD))
    table, passed = lax.optimization_barrier((table, passed))
    other = lax.ppermute(table, "core", [(0, 1), (1, 0)])
    sent = pl.pallas_call(
        lookup_kernel,
        out_shape=jax.ShapeDtypeStruct((SENDERS, 16, PART), f32),
        in_specs=[SCALARS] + [FULL] * 4,
        out_specs=FULL,
        compiler_params=PARAMS,
        name="lookup",
    )(where, slots, passed, table, other)
    received = lax.all_to_all(sent, ("y", "zh"), 0, 0)
    partial = pl.pallas_call(
        force_kernel,
        out_shape=jax.ShapeDtypeStruct((MEMBERS, 8, PART), f32),
        in_specs=[SCALARS] + [FULL] * 3,
        out_specs=FULL,
        scratch_shapes=[
            pltpu.VMEM((80, SOURCES), bf16),
            pltpu.VMEM((32, SOURCES), bf16),
            pltpu.VMEM((32, SOURCES), bf16),
            pltpu.VMEM((32, PART), f32),
            pltpu.VMEM((16, PART), f32),
        ],
        compiler_params=PARAMS,
        name="forces",
    )(where, received, table, other)
    shares = lax.all_to_all(partial, AXES, 0, 0, axis_index_groups=exchange_groups())
    half_result = pl.pallas_call(
        correct_kernel,
        out_shape=jax.ShapeDtypeStruct((12, HALF), f32),
        in_specs=[FULL],
        out_specs=FULL,
        compiler_params=PARAMS,
        name="corrector",
    )(shares)
    halves = lax.all_gather(half_result, "core")
    result = jnp.concatenate([halves[0], halves[1]], 1)
    return jnp.where((active_slots >= 0)[None, :], result, 0.0)


def solution(mesh):
    split_mesh = Mesh(mesh.devices.reshape(SIZES), AXES)
    return jax.shard_map(
        local,
        mesh=split_mesh,
        in_specs=(P(None, BLK), P(BLK), P(BLK), P(ACT)),
        out_specs=P(None, ACT),
        check_vma=False,
    )
```

```python
import functools

import jax
import jax.numpy as jnp
from jax import lax
from jax.experimental import pallas as pl
from jax.experimental.pallas import tpu as pltpu
from jax.sharding import Mesh, PartitionSpec as P

SOFTENING = 0.0025
STARS = 131072
ONE_THIRD = 1.0 / 3.0
ONE_TWELFTH = 1.0 / 12.0
bf16 = jnp.bfloat16
f32 = jnp.float32
AXES = ("y", "zh", "core", "xh", "xl", "zl")
SIZES = (4, 2, 2, 2, 2, 8)
BLK = ("y", "zh", "core")
ACT = ("xh", "xl", "zl")
SHARD = 8192
HALF = 512
PART = 256
SENDERS = 8
MEMBERS = 16
NEAR = 8
Y_ORDER = (2, 1, 3, 0)
CHUNK = 512
SOURCES = 2 * SHARD
FULL = pl.BlockSpec(memory_space=pltpu.VMEM)
SCALARS = pl.BlockSpec(memory_space=pltpu.SMEM)
PARAMS = pltpu.CompilerParams(vmem_limit_bytes=48 * 2**20)
NN = (((1,), (0,)), ((), ()))
TN = (((0,), (0,)), ((), ()))
dot = functools.partial(lax.dot_general, preferred_element_type=f32)


def exchange_groups(columns_of):
    groups = []
    for core in range(2):
        for columns in columns_of:
            for zl in range(8):
                groups.append(
                    [
                        (((y * 2 + zh) * 2 + core) * 4 + column) * 8 + zl
                        for zh in ((1, 0) if zl < NEAR else (0, 1))
                        for y in Y_ORDER
                        for column in columns
                    ]
                )
    return groups


def sender_of(y, zh, zl):
    near = (zl < NEAR).astype(jnp.int32)
    place = sum(jnp.where(y == value, k, 0) for k, value in enumerate(Y_ORDER))
    return jnp.where(zh == near, 0, 4) + place


def rows_of(value):
    return lax.broadcasted_iota(jnp.int32, value.shape, 0)


def split(value):
    high = value.astype(bf16).astype(f32)
    rest = value - high
    middle = rest.astype(bf16).astype(f32)
    return high, middle, rest - middle


def high_low(value):
    high = value.astype(bf16)
    return high, (value - high.astype(f32)).astype(bf16)


def table_kernel(state_in, mass_in, level_in, table, state, mass, level, done):
    copies = [
        pltpu.make_async_copy(source, target, done.at[k])
        for k, (source, target) in enumerate(
            ((state_in, state), (mass_in, mass), (level_in, level))
        )
    ]
    for copy in copies:
        copy.start()
    for copy in copies:
        copy.wait()
    lev = level[...]
    dt = jnp.where(lev == 0, 0.375, jnp.where(lev == 3, 0.0625, 0.125)).astype(f32)
    x, v, a, j = state[0:3], state[3:6], state[6:9], state[9:12]
    place = x + dt * (v + dt * 0.5 * (a + dt * ONE_THIRD * j))
    speed = v + dt * (a + dt * 0.5 * j)
    step_sq = dt * dt * ONE_TWELFTH
    half = 0.5 * dt
    table[0:3, :] = place
    table[3:6, :] = speed
    table[6:7, :] = mass[...]
    table[7:8, :] = dt
    table[8:11, :] = x + half * v + step_sq * a
    table[11:14, :] = v + half * a + step_sq * j
    table[14:15, :] = jnp.sum(place * place, 0, keepdims=True)
    table[15:16, :] = 3.0 * jnp.sum(place * speed, 0, keepdims=True)


def lookup_kernel(where, own_slots, passed_slots, mine, other, out):
    first, core, helper = where[0], where[1], where[2]
    at = pl.ds(core * 4 + helper * 2, 2)
    index = jnp.where(helper == 0, own_slots[at, :], passed_slots[at, :])
    index = jnp.concatenate((index[0:1], index[1:2]), 1)
    picked = jnp.zeros((16, PART), f32)
    for table, start in ((mine, first + core * SHARD), (other, first + (1 - core) * SHARD)):
        local_index = index - start
        low, high = local_index & 127, local_index >> 7
        low = jnp.broadcast_to(low, (128, PART))
        hit = jnp.where(rows_of(low) == low, 1.0, 0.0).astype(bf16)
        hits = jnp.concatenate((hit, hit, hit), 0)
        high = jnp.broadcast_to(high, (16, PART))
        for block in range(SHARD // 2048):
            tiles = [
                table[:, (block * 16 + i) * 128 : (block * 16 + i + 1) * 128] for i in range(16)
            ]
            parts = [part.astype(bf16) for part in split(jnp.concatenate(tiles, 0))]
            found = dot(jnp.concatenate(parts, 1), hits, NN)
            for i in range(16):
                picked = jnp.where(high == block * 16 + i, found[16 * i : 16 * i + 16], picked)
    for member in range(SENDERS):
        out[member] = picked


def source_features(table, features, pull, swing, offset):
    def step(turn, _):
        at = pl.ds(pl.multiple_of(turn * CHUNK, CHUNK), CHUNK)
        to = pl.ds(pl.multiple_of(offset + turn * CHUNK, CHUNK), CHUNK)
        upper, lower = table[0:8, at], table[8:16, at]
        row = rows_of(upper)
        a, b, c = split(jnp.where(row == 7, 1.0, upper))
        d, e, f = split(lower)
        zero = jnp.zeros_like(a)
        pairs = ((a, a), (a, b), (b, c), (d, e), (f, zero))
        for k, pair in enumerate(pairs):
            features[16 * k : 16 * k + 16, to] = jnp.concatenate(pair, 0).astype(bf16)
        weight = upper[6:7] * (1.0 / STARS)
        moved = jnp.where(row == 7, 0.0, jnp.where(row == 6, 1.0, upper)) * weight
        placed = pltpu.roll(moved, 3, 0)
        turned = jnp.where(row == 7, weight, jnp.where((row >= 3) & (row < 6), -placed, 0.0))
        for ref, value in ((pull, moved), (swing, turned)):
            a, b, c = split(value)
            ref[0:16, to] = jnp.concatenate((a, b), 0).astype(bf16)
            ref[16:32, to] = jnp.concatenate((c, zero), 0).astype(bf16)
        return 0

    lax.fori_loop(0, SHARD // CHUNK, step, 0)


def target_features(target):
    row = rows_of(target)
    place = jnp.where(row < 3, target, 0.0)
    speed = pltpu.roll(target, 5, 0)
    place_sq = jnp.sum(place * place, 0, keepdims=True) + SOFTENING
    product = 3.0 * jnp.sum(place * speed, 0, keepdims=True)
    shifted = pltpu.roll(target, 3, 0)
    radius = jnp.where(row == 7, place_sq, -2.0 * place)
    near = jnp.where(
        row == 7,
        product,
        jnp.where(row < 3, -3.0 * speed, jnp.where(row < 6, -3.0 * shifted, 0.0)),
    )
    zero = jnp.zeros_like(target)
    result = []
    for value, own_row in ((radius, 6), (near, 7)):
        a, b, c = split(value)
        one = jnp.where(row == own_row, 1.0, 0.0)
        result.append(
            jnp.concatenate((a, b, c, a, b, a, one, one, one, zero), 0).astype(bf16)
        )
    return result


def force_kernel(where, received, mine, other, out, features, pull, swing, total, rows):
    target_rows = received[0]
    for sender in range(1, SENDERS):
        target_rows = target_rows + received[sender]
    target = target_rows[0:8]
    rows[...] = target_rows
    source_features(mine, features, pull, swing, 0)
    source_features(other, features, pull, swing, SHARD)
    radius_part, near_part = target_features(target)
    total[...] = jnp.zeros_like(total)

    def step(turn, _):
        at = pl.ds(pl.multiple_of(turn * CHUNK, CHUNK), CHUNK)
        source = features[:, at]
        radius_sq = dot(source, radius_part, TN)
        product = dot(source, near_part, TN)
        inverse = lax.rsqrt(radius_sq)
        inverse_sq = inverse * inverse
        strength = inverse_sq * inverse
        turning = (product * inverse_sq) * strength
        pulls, swings = pull[:, at], swing[:, at]
        total[...] += dot(
            jnp.concatenate((pulls, pulls, swings, swings), 1),
            jnp.concatenate(high_low(strength) + high_low(turning), 0),
            NN,
        )
        return 0

    lax.fori_loop(0, SOURCES // CHUNK, step, 0, unroll=16)
    sums = total[0:8] + total[8:16] + total[16:24]
    place, speed = target[0:3], target[3:6]
    accel = sums[0:3] - place * sums[6:7]
    jerk = sums[3:6] - speed * sums[6:7] + place * sums[7:8]
    spare = rows[pl.ds(7 + where[3], 1), :]
    for member in range(MEMBERS):
        out[member, 0:3, :] = accel
        out[member, 3:6, :] = jerk
        out[member, 6:7, :] = spare
        out[member, 7:8, :] = spare


def correct_kernel(received, out):
    for part in range(2):
        force = received[part]
        for sender in range(1, SENDERS):
            force = force + received[2 * sender + part]
        dt = received[part, 6:7, :]
        bases = [received[2 * sender + part, 6:7, :] for sender in range(1, 7)]
        accel, jerk = force[0:3], force[3:6]
        half = 0.5 * dt
        step_sq = dt * dt * ONE_TWELFTH
        velocity = jnp.concatenate(bases[3:6], 0) + half * accel - step_sq * jerk
        position = jnp.concatenate(bases[0:3], 0) + half * velocity - step_sq * accel
        at = slice(part * PART, (part + 1) * PART)
        out[0:3, at] = position
        out[3:6, at] = velocity
        out[6:9, at] = accel
        out[9:12, at] = jerk


def local(star_state, star_mass, star_level, active_slots):
    core, helper = lax.axis_index("core"), lax.axis_index("xh")
    y, zh = lax.axis_index("y"), lax.axis_index("zh")
    sender = sender_of(y, zh, lax.axis_index("zl"))
    where = jnp.stack([(y * 2 + zh) * SOURCES, core, helper, sender]).astype(jnp.int32)
    slots = active_slots.reshape(8, 128)
    passed = lax.ppermute(slots, ("xh", "xl"), [(x, 3 - x) for x in range(4)])
    anywhere = pl.BlockSpec(memory_space=pl.ANY)
    table = pl.pallas_call(
        table_kernel,
        out_shape=jax.ShapeDtypeStruct((16, SHARD), f32),
        in_specs=[anywhere] * 3,
        out_specs=FULL,
        scratch_shapes=[
            pltpu.VMEM((12, SHARD), f32),
            pltpu.VMEM((1, SHARD), f32),
            pltpu.VMEM((1, SHARD), jnp.int32),
            pltpu.SemaphoreType.DMA((3,)),
        ],
        compiler_params=PARAMS,
        cost_estimate=pl.CostEstimate(
            flops=10**10, bytes_accessed=120 * SHARD, transcendentals=0
        ),
        name="table",
    )(star_state, star_mass.reshape(1, SHARD), star_level.reshape(1, SHARD))
    table, passed = lax.optimization_barrier((table, passed))
    other = lax.ppermute(table, "core", [(0, 1), (1, 0)])
    sent = pl.pallas_call(
        lookup_kernel,
        out_shape=jax.ShapeDtypeStruct((SENDERS, 16, PART), f32),
        in_specs=[SCALARS] + [FULL] * 4,
        out_specs=FULL,
        compiler_params=PARAMS,
        name="lookup",
    )(where, slots, passed, table, other)
    alone = exchange_groups([(x,) for x in range(4)])
    received = lax.all_to_all(sent, AXES, 0, 0, axis_index_groups=alone)
    partial = pl.pallas_call(
        force_kernel,
        out_shape=jax.ShapeDtypeStruct((MEMBERS, 8, PART), f32),
        in_specs=[SCALARS] + [FULL] * 3,
        out_specs=FULL,
        scratch_shapes=[
            pltpu.VMEM((80, SOURCES), bf16),
            pltpu.VMEM((32, SOURCES), bf16),
            pltpu.VMEM((32, SOURCES), bf16),
            pltpu.VMEM((32, PART), f32),
            pltpu.VMEM((16, PART), f32),
        ],
        compiler_params=PARAMS,
        name="forces",
    )(where, received, table, other)
    paired = exchange_groups([(x, 3 - x) for x in range(2)])
    shares = lax.all_to_all(partial, AXES, 0, 0, axis_index_groups=paired)
    half_result = pl.pallas_call(
        correct_kernel,
        out_shape=jax.ShapeDtypeStruct((12, HALF), f32),
        in_specs=[FULL],
        out_specs=FULL,
        compiler_params=PARAMS,
        name="corrector",
    )(shares)
    halves = lax.all_gather(half_result, "core")
    result = jnp.concatenate([halves[0], halves[1]], 1)
    return jnp.where((active_slots >= 0)[None, :], result, 0.0)


def solution(mesh):
    split_mesh = Mesh(mesh.devices.reshape(SIZES), AXES)
    return jax.shard_map(
        local,
        mesh=split_mesh,
        in_specs=(P(None, BLK), P(BLK), P(BLK), P(ACT)),
        out_specs=P(None, ACT),
        check_vma=False,
    )
```

```python
import functools

import jax
import jax.numpy as jnp
from jax import lax
from jax.experimental import pallas as pl
from jax.experimental.pallas import tpu as pltpu
from jax.sharding import Mesh, PartitionSpec as P

SOFTENING = 0.0025
STARS = 131072
ONE_THIRD = 1.0 / 3.0
ONE_TWELFTH = 1.0 / 12.0
bf16 = jnp.bfloat16
f32 = jnp.float32
AXES = ("y", "zh", "core", "xh", "xl", "zl")
SIZES = (4, 2, 2, 2, 2, 8)
BLK = ("y", "zh", "core")
ACT = ("xh", "xl", "zl")
SHARD = 8192
HALF = 512
PART = 256
SENDERS = 8
MEMBERS = 16
NEAR = 8
Y_ORDER = (2, 1, 3, 0)
CHUNK = 512
UNROLL = 16
SOURCES = 2 * SHARD
FULL = pl.BlockSpec(memory_space=pltpu.VMEM)
SCALARS = pl.BlockSpec(memory_space=pltpu.SMEM)
PARAMS = pltpu.CompilerParams(vmem_limit_bytes=48 * 2**20)
LONG = pl.CostEstimate(flops=10**10, bytes_accessed=2**24, transcendentals=0)
NN = (((1,), (0,)), ((), ()))
TN = (((0,), (0,)), ((), ()))
dot = functools.partial(lax.dot_general, preferred_element_type=f32)


def exchange_groups(columns_of):
    groups = []
    for core in range(2):
        for columns in columns_of:
            for zl in range(8):
                groups.append(
                    [
                        (((y * 2 + zh) * 2 + core) * 4 + column) * 8 + zl
                        for zh in ((1, 0) if zl < NEAR else (0, 1))
                        for y in Y_ORDER
                        for column in columns
                    ]
                )
    return groups


def sender_of(y, zh, zl):
    near = (zl < NEAR).astype(jnp.int32)
    place = sum(jnp.where(y == value, k, 0) for k, value in enumerate(Y_ORDER))
    return jnp.where(zh == near, 0, 4) + place


def rows_of(value):
    return lax.broadcasted_iota(jnp.int32, value.shape, 0)


def split(value):
    high = value.astype(bf16).astype(f32)
    rest = value - high
    middle = rest.astype(bf16).astype(f32)
    return high, middle, rest - middle


def high_low(value):
    high = value.astype(bf16)
    return high, (value - high.astype(f32)).astype(bf16)


def slots_kernel(slots_in, slots):
    slots[...] = slots_in[...]


def index_kernel(where, own_slots, passed_slots, index):
    core, helper = where[1], where[2]
    at = pl.ds(core * 4 + helper * 2, 2)
    chosen = jnp.where(helper == 0, own_slots[at, :], passed_slots[at, :])
    index[...] = jnp.concatenate((chosen[0:1], chosen[1:2]), 1)


def table_kernel(state_in, mass_in, level_in, table, state, mass, level, done):
    copies = [
        pltpu.make_async_copy(source, target, done.at[k])
        for k, (source, target) in enumerate(
            ((state_in, state), (mass_in, mass), (level_in, level))
        )
    ]
    for copy in copies:
        copy.start()
    for copy in copies:
        copy.wait()
    lev = level[...]
    dt = jnp.where(lev == 0, 0.375, jnp.where(lev == 3, 0.0625, 0.125)).astype(f32)
    x, v, a, j = state[0:3], state[3:6], state[6:9], state[9:12]
    place = x + dt * (v + dt * 0.5 * (a + dt * ONE_THIRD * j))
    speed = v + dt * (a + dt * 0.5 * j)
    step_sq = dt * dt * ONE_TWELFTH
    half = 0.5 * dt
    table[0:3, :] = place
    table[3:6, :] = speed
    table[6:7, :] = mass[...]
    table[7:8, :] = dt
    table[8:11, :] = x + half * v + step_sq * a
    table[11:14, :] = v + half * a + step_sq * j
    table[14:15, :] = jnp.sum(place * place, 0, keepdims=True)
    table[15:16, :] = 3.0 * jnp.sum(place * speed, 0, keepdims=True)


def lookup_kernel(where, index_in, mine, other, out):
    first, core = where[0], where[1]
    index = index_in[...]
    picked = jnp.zeros((16, PART), f32)
    for table, start in ((mine, first + core * SHARD), (other, first + (1 - core) * SHARD)):
        local_index = index - start
        low, high = local_index & 127, local_index >> 7
        low = jnp.broadcast_to(low, (128, PART))
        hit = jnp.where(rows_of(low) == low, 1.0, 0.0).astype(bf16)
        hits = jnp.concatenate((hit, hit, hit), 0)
        high = jnp.broadcast_to(high, (16, PART))
        for block in range(SHARD // 2048):
            tiles = [
                table[:, (block * 16 + i) * 128 : (block * 16 + i + 1) * 128] for i in range(16)
            ]
            parts = [part.astype(bf16) for part in split(jnp.concatenate(tiles, 0))]
            found = dot(jnp.concatenate(parts, 1), hits, NN)
            for i in range(16):
                picked = jnp.where(high == block * 16 + i, found[16 * i : 16 * i + 16], picked)
    for member in range(SENDERS):
        out[member] = picked


def source_features(upper, lower):
    row = rows_of(upper)
    a, b, c = split(jnp.where(row == 7, 1.0, upper))
    d, e, f = split(lower)
    zero = jnp.zeros_like(a)
    features = jnp.concatenate((a, a, a, b, b, c, d, e, f, zero), 0).astype(bf16)
    weight = upper[6:7] * (1.0 / STARS)
    moved = jnp.where(row == 7, 0.0, jnp.where(row == 6, 1.0, upper)) * weight
    placed = pltpu.roll(moved, 3, 0)
    turned = jnp.where(row == 7, weight, jnp.where((row >= 3) & (row < 6), -placed, 0.0))
    pull, swing = [
        jnp.concatenate(split(value) + (zero,), 0).astype(bf16) for value in (moved, turned)
    ]
    return features, pull, swing


def target_features(target):
    row = rows_of(target)
    place = jnp.where(row < 3, target, 0.0)
    speed = pltpu.roll(target, 5, 0)
    place_sq = jnp.sum(place * place, 0, keepdims=True) + SOFTENING
    product = 3.0 * jnp.sum(place * speed, 0, keepdims=True)
    shifted = pltpu.roll(target, 3, 0)
    radius = jnp.where(row == 7, place_sq, -2.0 * place)
    near = jnp.where(
        row == 7,
        product,
        jnp.where(row < 3, -3.0 * speed, jnp.where(row < 6, -3.0 * shifted, 0.0)),
    )
    zero = jnp.zeros_like(target)
    result = []
    for value, own_row in ((radius, 6), (near, 7)):
        a, b, c = split(value)
        one = jnp.where(row == own_row, 1.0, 0.0)
        result.append(
            jnp.concatenate((a, b, c, a, b, a, one, one, one, zero), 0).astype(bf16)
        )
    return result


def force_kernel(where, received, mine, other, out, total, rows):
    target_rows = received[0]
    for sender in range(1, SENDERS):
        target_rows = target_rows + received[sender]
    target = target_rows[0:8]
    rows[...] = target_rows
    radius_part, near_part = target_features(target)
    total[...] = jnp.zeros_like(total)
    for table in (mine, other):

        def step(turn, _):
            at = pl.ds(pl.multiple_of(turn * CHUNK, CHUNK), CHUNK)
            source, pull, swing = source_features(table[0:8, at], table[8:16, at])
            radius_sq = dot(source, radius_part, TN)
            product = dot(source, near_part, TN)
            inverse = lax.rsqrt(radius_sq)
            inverse_sq = inverse * inverse
            strength = inverse_sq * inverse
            turning = (product * inverse_sq) * strength
            total[...] += dot(
                jnp.concatenate((pull, pull, swing, swing), 1),
                jnp.concatenate(high_low(strength) + high_low(turning), 0),
                NN,
            )
            return 0

        lax.fori_loop(0, SHARD // CHUNK, step, 0, unroll=UNROLL)
    sums = total[0:8] + total[8:16] + total[16:24]
    place, speed = target[0:3], target[3:6]
    accel = sums[0:3] - place * sums[6:7]
    jerk = sums[3:6] - speed * sums[6:7] + place * sums[7:8]
    spare = rows[pl.ds(7 + where[3], 1), :]
    for member in range(MEMBERS):
        out[member, 0:3, :] = accel
        out[member, 3:6, :] = jerk
        out[member, 6:7, :] = spare
        out[member, 7:8, :] = spare


def correct_kernel(received, out):
    for part in range(2):
        force = received[part]
        for sender in range(1, SENDERS):
            force = force + received[2 * sender + part]
        dt = received[part, 6:7, :]
        bases = [received[2 * sender + part, 6:7, :] for sender in range(1, 7)]
        accel, jerk = force[0:3], force[3:6]
        half = 0.5 * dt
        step_sq = dt * dt * ONE_TWELFTH
        velocity = jnp.concatenate(bases[3:6], 0) + half * accel - step_sq * jerk
        position = jnp.concatenate(bases[0:3], 0) + half * velocity - step_sq * accel
        at = slice(part * PART, (part + 1) * PART)
        out[0:3, at] = position
        out[3:6, at] = velocity
        out[6:9, at] = accel
        out[9:12, at] = jerk


def local(star_state, star_mass, star_level, active_slots):
    core, helper = lax.axis_index("core"), lax.axis_index("xh")
    y, zh = lax.axis_index("y"), lax.axis_index("zh")
    sender = sender_of(y, zh, lax.axis_index("zl"))
    where = jnp.stack([(y * 2 + zh) * SOURCES, core, helper, sender]).astype(jnp.int32)
    slots = pl.pallas_call(
        slots_kernel,
        out_shape=jax.ShapeDtypeStruct((8, 128), jnp.int32),
        in_specs=[FULL],
        out_specs=FULL,
        compiler_params=PARAMS,
        cost_estimate=LONG,
        name="slots",
    )(active_slots.reshape(8, 128))
    passed = lax.ppermute(slots, ("xh", "xl"), [(x, 3 - x) for x in range(4)])
    anywhere = pl.BlockSpec(memory_space=pl.ANY)
    table = pl.pallas_call(
        table_kernel,
        out_shape=jax.ShapeDtypeStruct((16, SHARD), f32),
        in_specs=[anywhere] * 3,
        out_specs=FULL,
        scratch_shapes=[
            pltpu.VMEM((12, SHARD), f32),
            pltpu.VMEM((1, SHARD), f32),
            pltpu.VMEM((1, SHARD), jnp.int32),
            pltpu.SemaphoreType.DMA((3,)),
        ],
        compiler_params=PARAMS,
        cost_estimate=LONG,
        name="table",
    )(star_state, star_mass.reshape(1, SHARD), star_level.reshape(1, SHARD))
    other = lax.ppermute(table, "core", [(0, 1), (1, 0)])
    index = pl.pallas_call(
        index_kernel,
        out_shape=jax.ShapeDtypeStruct((1, PART), jnp.int32),
        in_specs=[SCALARS] + [FULL] * 2,
        out_specs=FULL,
        compiler_params=PARAMS,
        cost_estimate=LONG,
        name="index",
    )(where, slots, passed)
    sent = pl.pallas_call(
        lookup_kernel,
        out_shape=jax.ShapeDtypeStruct((SENDERS, 16, PART), f32),
        in_specs=[SCALARS] + [FULL] * 3,
        out_specs=FULL,
        compiler_params=PARAMS,
        name="lookup",
    )(where, index, table, other)
    alone = exchange_groups([(x,) for x in range(4)])
    received = lax.all_to_all(sent, AXES, 0, 0, axis_index_groups=alone)
    partial = pl.pallas_call(
        force_kernel,
        out_shape=jax.ShapeDtypeStruct((MEMBERS, 8, PART), f32),
        in_specs=[SCALARS] + [FULL] * 3,
        out_specs=FULL,
        scratch_shapes=[
            pltpu.VMEM((32, PART), f32),
            pltpu.VMEM((16, PART), f32),
        ],
        compiler_params=PARAMS,
        name="forces",
    )(where, received, table, other)
    paired = exchange_groups([(x, 3 - x) for x in range(2)])
    shares = lax.all_to_all(partial, AXES, 0, 0, axis_index_groups=paired)
    half_result = pl.pallas_call(
        correct_kernel,
        out_shape=jax.ShapeDtypeStruct((12, HALF), f32),
        in_specs=[FULL],
        out_specs=FULL,
        compiler_params=PARAMS,
        name="corrector",
    )(shares)
    halves = lax.all_gather(half_result, "core")
    result = jnp.concatenate([halves[0], halves[1]], 1)
    return jnp.where((active_slots >= 0)[None, :], result, 0.0)


def solution(mesh):
    split_mesh = Mesh(mesh.devices.reshape(SIZES), AXES)
    return jax.shard_map(
        local,
        mesh=split_mesh,
        in_specs=(P(None, BLK), P(BLK), P(BLK), P(ACT)),
        out_specs=P(None, ACT),
        check_vma=False,
    )
```

```python
import functools

import jax
import jax.numpy as jnp
from jax import lax
from jax.experimental import pallas as pl
from jax.experimental.pallas import tpu as pltpu
from jax.sharding import Mesh, PartitionSpec as P

SOFTENING = 0.0025
STARS = 131072
ONE_THIRD = 1.0 / 3.0
ONE_TWELFTH = 1.0 / 12.0
bf16 = jnp.bfloat16
f32 = jnp.float32
AXES = ("y", "zh", "core", "xh", "xl", "zl")
SIZES = (4, 2, 2, 2, 2, 8)
BLK = ("y", "zh", "core")
ACT = ("xh", "xl", "zl")
SHARD = 8192
ROWS = 15
HALF = 512
PART = 256
SENDERS = 8
MEMBERS = 16
NEAR = 8
Y_ORDER = (2, 1, 3, 0)
CHUNK = 512
UNROLL = 16
SOURCES = 2 * SHARD
FULL = pl.BlockSpec(memory_space=pltpu.VMEM)
SCALARS = pl.BlockSpec(memory_space=pltpu.SMEM)
PARAMS = pltpu.CompilerParams(vmem_limit_bytes=48 * 2**20)
LONG = pl.CostEstimate(flops=10**10, bytes_accessed=2**24, transcendentals=0)
NN = (((1,), (0,)), ((), ()))
TN = (((0,), (0,)), ((), ()))
dot = functools.partial(lax.dot_general, preferred_element_type=f32)


def exchange_groups(columns_of):
    groups = []
    for core in range(2):
        for columns in columns_of:
            for zl in range(8):
                groups.append(
                    [
                        (((y * 2 + zh) * 2 + core) * 4 + column) * 8 + zl
                        for zh in ((1, 0) if zl < NEAR else (0, 1))
                        for y in Y_ORDER
                        for column in columns
                    ]
                )
    return groups


def sender_of(y, zh, zl):
    near = (zl < NEAR).astype(jnp.int32)
    place = sum(jnp.where(y == value, k, 0) for k, value in enumerate(Y_ORDER))
    return jnp.where(zh == near, 0, 4) + place


def rows_of(value):
    return lax.broadcasted_iota(jnp.int32, value.shape, 0)


def split(value):
    high = value.astype(bf16).astype(f32)
    rest = value - high
    middle = rest.astype(bf16).astype(f32)
    return high, middle, rest - middle


def high_low(value):
    high = value.astype(bf16)
    return high, (value - high.astype(f32)).astype(bf16)


def slots_kernel(slots_in, slots):
    slots[...] = slots_in[...]


def table_kernel(state_in, mass_in, level_in, table, state, mass, level, done):
    copies = [
        pltpu.make_async_copy(source, target, done.at[k])
        for k, (source, target) in enumerate(
            ((state_in, state), (mass_in, mass), (level_in, level))
        )
    ]
    for copy in copies:
        copy.start()
    for copy in copies:
        copy.wait()
    lev = level[...]
    dt = jnp.where(lev == 0, 0.375, jnp.where(lev == 3, 0.0625, 0.125)).astype(f32)
    x, v, a, j = state[0:3], state[3:6], state[6:9], state[9:12]
    place = x + dt * (v + dt * 0.5 * (a + dt * ONE_THIRD * j))
    speed = v + dt * (a + dt * 0.5 * j)
    step_sq = dt * dt * ONE_TWELFTH
    half = 0.5 * dt
    table[0:3, :] = place
    table[3:6, :] = speed
    table[6:7, :] = mass[...]
    table[7:8, :] = dt
    table[8:11, :] = x + half * v + step_sq * a
    table[11:14, :] = v + half * a + step_sq * j
    table[14:15, :] = jnp.sum(place * place, 0, keepdims=True)


def lookup_kernel(where, own_slots, passed_slots, tables, out):
    first, core, helper = where[0], where[1], where[2]
    at = pl.ds(core * 4 + helper * 2, 2)
    index = jnp.where(helper == 0, own_slots[at, :], passed_slots[at, :])
    index = jnp.concatenate((index[0:1], index[1:2]), 1)
    picked = jnp.zeros((16, PART), f32)
    spare = jnp.zeros((16 - ROWS, 128), f32)
    for k in range(2):
        local_index = index - (first + k * SHARD)
        low, high = local_index & 127, local_index >> 7
        low = jnp.broadcast_to(low, (128, PART))
        hit = jnp.where(rows_of(low) == low, 1.0, 0.0).astype(bf16)
        hits = jnp.concatenate((hit, hit, hit), 0)
        high = jnp.broadcast_to(high, (16, PART))
        for block in range(SHARD // 2048):
            tiles = []
            for i in range(block * 16, block * 16 + 16):
                tiles += [tables[k, :, i * 128 : (i + 1) * 128], spare]
            parts = [part.astype(bf16) for part in split(jnp.concatenate(tiles, 0))]
            found = dot(jnp.concatenate(parts, 1), hits, NN)
            for i in range(16):
                picked = jnp.where(high == block * 16 + i, found[16 * i : 16 * i + 16], picked)
    for member in range(SENDERS):
        out[member] = picked


def source_features(upper, place_sq):
    row = rows_of(upper)
    speed = pltpu.roll(upper, 5, 0)
    product = 3.0 * jnp.sum(jnp.where(row < 3, upper * speed, 0.0), 0, keepdims=True)
    a, b, c = split(jnp.where(row == 7, 1.0, upper))
    d, e, f = split(jnp.where(row == 6, place_sq, jnp.where(row == 7, product, 0.0)))
    zero = jnp.zeros_like(a)
    features = jnp.concatenate((a, a, a, b, b, c, d, e, f, zero), 0).astype(bf16)
    weight = upper[6:7] * (1.0 / STARS)
    moved = jnp.where(row == 7, 0.0, jnp.where(row == 6, 1.0, upper)) * weight
    placed = pltpu.roll(moved, 3, 0)
    turned = jnp.where(row == 7, weight, jnp.where((row >= 3) & (row < 6), -placed, 0.0))
    pull, swing = [
        jnp.concatenate(split(value) + (zero,), 0).astype(bf16) for value in (moved, turned)
    ]
    return features, pull, swing


def target_features(target):
    row = rows_of(target)
    place = jnp.where(row < 3, target, 0.0)
    speed = pltpu.roll(target, 5, 0)
    place_sq = jnp.sum(place * place, 0, keepdims=True) + SOFTENING
    product = 3.0 * jnp.sum(place * speed, 0, keepdims=True)
    shifted = pltpu.roll(target, 3, 0)
    radius = jnp.where(row == 7, place_sq, -2.0 * place)
    near = jnp.where(
        row == 7,
        product,
        jnp.where(row < 3, -3.0 * speed, jnp.where(row < 6, -3.0 * shifted, 0.0)),
    )
    zero = jnp.zeros_like(target)
    result = []
    for value, own_row in ((radius, 6), (near, 7)):
        a, b, c = split(value)
        one = jnp.where(row == own_row, 1.0, 0.0)
        result.append(
            jnp.concatenate((a, b, c, a, b, a, one, one, one, zero), 0).astype(bf16)
        )
    return result


def force_kernel(where, received, tables, out, total, rows):
    target_rows = received[0]
    for sender in range(1, SENDERS):
        target_rows = target_rows + received[sender]
    target = target_rows[0:8]
    rows[...] = target_rows
    radius_part, near_part = target_features(target)
    total[...] = jnp.zeros_like(total)
    for k in range(2):

        def step(turn, _, k=k):
            at = pl.ds(pl.multiple_of(turn * CHUNK, CHUNK), CHUNK)
            source, pull, swing = source_features(tables[k, 0:8, at], tables[k, 14:15, at])
            radius_sq = dot(source, radius_part, TN)
            product = dot(source, near_part, TN)
            inverse = lax.rsqrt(radius_sq)
            inverse_sq = inverse * inverse
            strength = inverse_sq * inverse
            turning = (product * inverse_sq) * strength
            total[...] += dot(
                jnp.concatenate((pull, pull, swing, swing), 1),
                jnp.concatenate(high_low(strength) + high_low(turning), 0),
                NN,
            )
            return 0

        lax.fori_loop(0, SHARD // CHUNK, step, 0, unroll=UNROLL)
    sums = total[0:8] + total[8:16] + total[16:24]
    place, speed = target[0:3], target[3:6]
    accel = sums[0:3] - place * sums[6:7]
    jerk = sums[3:6] - speed * sums[6:7] + place * sums[7:8]
    spare = rows[pl.ds(7 + where[3], 1), :]
    for member in range(MEMBERS):
        out[member, 0:3, :] = accel
        out[member, 3:6, :] = jerk
        out[member, 6:7, :] = spare
        out[member, 7:8, :] = spare


def correct_kernel(received, out):
    for part in range(2):
        force = received[part]
        for sender in range(1, SENDERS):
            force = force + received[2 * sender + part]
        dt = received[part, 6:7, :]
        bases = [received[2 * sender + part, 6:7, :] for sender in range(1, 7)]
        accel, jerk = force[0:3], force[3:6]
        half = 0.5 * dt
        step_sq = dt * dt * ONE_TWELFTH
        velocity = jnp.concatenate(bases[3:6], 0) + half * accel - step_sq * jerk
        position = jnp.concatenate(bases[0:3], 0) + half * velocity - step_sq * accel
        at = slice(part * PART, (part + 1) * PART)
        out[0:3, at] = position
        out[3:6, at] = velocity
        out[6:9, at] = accel
        out[9:12, at] = jerk


def local(star_state, star_mass, star_level, active_slots):
    core, helper = lax.axis_index("core"), lax.axis_index("xh")
    y, zh = lax.axis_index("y"), lax.axis_index("zh")
    sender = sender_of(y, zh, lax.axis_index("zl"))
    where = jnp.stack([(y * 2 + zh) * SOURCES, core, helper, sender]).astype(jnp.int32)
    slots = pl.pallas_call(
        slots_kernel,
        out_shape=jax.ShapeDtypeStruct((8, 128), jnp.int32),
        in_specs=[FULL],
        out_specs=FULL,
        compiler_params=PARAMS,
        cost_estimate=LONG,
        name="slots",
    )(active_slots.reshape(8, 128))
    passed = lax.ppermute(slots, ("xh", "xl"), [(x, 3 - x) for x in range(4)])
    anywhere = pl.BlockSpec(memory_space=pl.ANY)
    table = pl.pallas_call(
        table_kernel,
        out_shape=jax.ShapeDtypeStruct((ROWS, SHARD), f32),
        in_specs=[anywhere] * 3,
        out_specs=FULL,
        scratch_shapes=[
            pltpu.VMEM((12, SHARD), f32),
            pltpu.VMEM((1, SHARD), f32),
            pltpu.VMEM((1, SHARD), jnp.int32),
            pltpu.SemaphoreType.DMA((3,)),
        ],
        compiler_params=PARAMS,
        cost_estimate=LONG,
        name="table",
    )(star_state, star_mass.reshape(1, SHARD), star_level.reshape(1, SHARD))
    tables = lax.all_gather(table, "core")
    sent = pl.pallas_call(
        lookup_kernel,
        out_shape=jax.ShapeDtypeStruct((SENDERS, 16, PART), f32),
        in_specs=[SCALARS] + [FULL] * 3,
        out_specs=FULL,
        compiler_params=PARAMS,
        name="lookup",
    )(where, slots, passed, tables)
    alone = exchange_groups([(x,) for x in range(4)])
    received = lax.all_to_all(sent, AXES, 0, 0, axis_index_groups=alone)
    partial = pl.pallas_call(
        force_kernel,
        out_shape=jax.ShapeDtypeStruct((MEMBERS, 8, PART), f32),
        in_specs=[SCALARS] + [FULL] * 2,
        out_specs=FULL,
        scratch_shapes=[
            pltpu.VMEM((32, PART), f32),
            pltpu.VMEM((16, PART), f32),
        ],
        compiler_params=PARAMS,
        name="forces",
    )(where, received, tables)
    paired = exchange_groups([(x, 3 - x) for x in range(2)])
    shares = lax.all_to_all(partial, AXES, 0, 0, axis_index_groups=paired)
    half_result = pl.pallas_call(
        correct_kernel,
        out_shape=jax.ShapeDtypeStruct((12, HALF), f32),
        in_specs=[FULL],
        out_specs=FULL,
        compiler_params=PARAMS,
        name="corrector",
    )(shares)
    halves = lax.all_gather(half_result, "core")
    result = jnp.concatenate([halves[0], halves[1]], 1)
    return jnp.where((active_slots >= 0)[None, :], result, 0.0)


def solution(mesh):
    split_mesh = Mesh(mesh.devices.reshape(SIZES), AXES)
    return jax.shard_map(
        local,
        mesh=split_mesh,
        in_specs=(P(None, BLK), P(BLK), P(BLK), P(ACT)),
        out_specs=P(None, ACT),
        check_vma=False,
    )
```

```python
import functools

import jax
import jax.numpy as jnp
from jax import lax
from jax.experimental import pallas as pl
from jax.experimental.pallas import tpu as pltpu
from jax.sharding import Mesh, PartitionSpec as P

SOFTENING = 0.0025
STARS = 131072
ONE_THIRD = 1.0 / 3.0
ONE_TWELFTH = 1.0 / 12.0
bf16 = jnp.bfloat16
f32 = jnp.float32
AXES = ("y", "zh", "core", "xh", "xl", "zl")
SIZES = (4, 2, 2, 2, 2, 8)
BLK = ("y", "zh", "core")
ACT = ("xh", "xl", "zl")
SHARD = 8192
ROWS = 15
HALF = 512
PART = 256
SENDERS = 8
MEMBERS = 16
Y_ORDER = (2, 1, 3, 0)
ALONE = [(zh, y, 0) for zh in (1, 0) for y in Y_ORDER]
PAIRED = [(zh, y, role) for role in (1, 0) for zh in (1, 0) for y in Y_ORDER]
CHUNK = 512
UNROLL = 16
SOURCES = 2 * SHARD
FULL = pl.BlockSpec(memory_space=pltpu.VMEM)
SCALARS = pl.BlockSpec(memory_space=pltpu.SMEM)
PARAMS = pltpu.CompilerParams(vmem_limit_bytes=48 * 2**20)
LONG = pl.CostEstimate(flops=10**10, bytes_accessed=2**24, transcendentals=0)
NN = (((1,), (0,)), ((), ()))
TN = (((0,), (0,)), ((), ()))
dot = functools.partial(lax.dot_general, preferred_element_type=f32)


def exchange_groups(order, columns_of):
    return [
        [
            (((y * 2 + zh) * 2 + core) * 4 + columns[role]) * 8 + zl
            for zh, y, role in order
        ]
        for core in range(2)
        for columns in columns_of
        for zl in range(8)
    ]


def sender_of(y, zh):
    place = sum(jnp.where(y == value, k, 0) for k, value in enumerate(Y_ORDER))
    return (1 - zh) * 4 + place


def rows_of(value):
    return lax.broadcasted_iota(jnp.int32, value.shape, 0)


def split(value):
    high = value.astype(bf16).astype(f32)
    rest = value - high
    middle = rest.astype(bf16).astype(f32)
    return high, middle, rest - middle


def high_low(value):
    high = value.astype(bf16)
    return high, (value - high.astype(f32)).astype(bf16)


def slots_kernel(slots_in, slots):
    slots[...] = slots_in[...]


def table_kernel(state_in, mass_in, level_in, table, state, mass, level, done):
    copies = [
        pltpu.make_async_copy(source, target, done.at[k])
        for k, (source, target) in enumerate(
            ((state_in, state), (mass_in, mass), (level_in, level))
        )
    ]
    for copy in copies:
        copy.start()
    for copy in copies:
        copy.wait()
    lev = level[...]
    dt = jnp.where(lev == 0, 0.375, jnp.where(lev == 3, 0.0625, 0.125)).astype(f32)
    x, v, a, j = state[0:3], state[3:6], state[6:9], state[9:12]
    place = x + dt * (v + dt * 0.5 * (a + dt * ONE_THIRD * j))
    speed = v + dt * (a + dt * 0.5 * j)
    step_sq = dt * dt * ONE_TWELFTH
    half = 0.5 * dt
    table[0:3, :] = place
    table[3:6, :] = speed
    table[6:7, :] = mass[...]
    table[7:8, :] = dt
    table[8:11, :] = x + half * v + step_sq * a
    table[11:14, :] = v + half * a + step_sq * j
    table[14:15, :] = jnp.sum(place * place, 0, keepdims=True)


def lookup_kernel(where, own_slots, passed_slots, tables, out):
    first, core, helper = where[0], where[1], where[2]
    at = pl.ds(core * 4 + helper * 2, 2)
    index = jnp.where(helper == 0, own_slots[at, :], passed_slots[at, :])
    index = jnp.concatenate((index[0:1], index[1:2]), 1)
    picked = jnp.zeros((16, PART), f32)
    spare = jnp.zeros((16 - ROWS, 128), f32)
    for k in range(2):
        local_index = index - (first + k * SHARD)
        low, high = local_index & 127, local_index >> 7
        low = jnp.broadcast_to(low, (128, PART))
        hit = jnp.where(rows_of(low) == low, 1.0, 0.0).astype(bf16)
        hits = jnp.concatenate((hit, hit, hit), 0)
        high = jnp.broadcast_to(high, (16, PART))
        for block in range(SHARD // 2048):
            tiles = []
            for i in range(block * 16, block * 16 + 16):
                tiles += [tables[k, :, i * 128 : (i + 1) * 128], spare]
            parts = [part.astype(bf16) for part in split(jnp.concatenate(tiles, 0))]
            found = dot(jnp.concatenate(parts, 1), hits, NN)
            for i in range(16):
                picked = jnp.where(high == block * 16 + i, found[16 * i : 16 * i + 16], picked)
    for member in range(SENDERS):
        out[member] = picked


def source_features(upper, place_sq):
    row = rows_of(upper)
    speed = pltpu.roll(upper, 5, 0)
    product = 3.0 * jnp.sum(jnp.where(row < 3, upper * speed, 0.0), 0, keepdims=True)
    a, b, c = split(jnp.where(row == 7, 1.0, upper))
    d, e, f = split(jnp.where(row == 6, place_sq, jnp.where(row == 7, product, 0.0)))
    zero = jnp.zeros_like(a)
    features = jnp.concatenate((a, a, a, b, b, c, d, e, f, zero), 0).astype(bf16)
    weight = upper[6:7] * (1.0 / STARS)
    moved = jnp.where(row == 7, 0.0, jnp.where(row == 6, 1.0, upper)) * weight
    placed = pltpu.roll(moved, 3, 0)
    turned = jnp.where(row == 7, weight, jnp.where((row >= 3) & (row < 6), -placed, 0.0))
    pull, swing = [
        jnp.concatenate(split(value) + (zero,), 0).astype(bf16) for value in (moved, turned)
    ]
    return features, pull, swing


def target_features(target):
    row = rows_of(target)
    place = jnp.where(row < 3, target, 0.0)
    speed = pltpu.roll(target, 5, 0)
    place_sq = jnp.sum(place * place, 0, keepdims=True) + SOFTENING
    product = 3.0 * jnp.sum(place * speed, 0, keepdims=True)
    shifted = pltpu.roll(target, 3, 0)
    radius = jnp.where(row == 7, place_sq, -2.0 * place)
    near = jnp.where(
        row == 7,
        product,
        jnp.where(row < 3, -3.0 * speed, jnp.where(row < 6, -3.0 * shifted, 0.0)),
    )
    zero = jnp.zeros_like(target)
    result = []
    for value, own_row in ((radius, 6), (near, 7)):
        a, b, c = split(value)
        one = jnp.where(row == own_row, 1.0, 0.0)
        result.append(
            jnp.concatenate((a, b, c, a, b, a, one, one, one, zero), 0).astype(bf16)
        )
    return result


def force_kernel(where, received, tables, out, total, rows):
    target_rows = received[0]
    for sender in range(1, SENDERS):
        target_rows = target_rows + received[sender]
    target = target_rows[0:8]
    rows[...] = target_rows
    radius_part, near_part = target_features(target)
    total[...] = jnp.zeros_like(total)
    for k in range(2):

        def step(turn, _, k=k):
            at = pl.ds(pl.multiple_of(turn * CHUNK, CHUNK), CHUNK)
            source, pull, swing = source_features(tables[k, 0:8, at], tables[k, 14:15, at])
            radius_sq = dot(source, radius_part, TN)
            product = dot(source, near_part, TN)
            inverse = lax.rsqrt(radius_sq)
            inverse_sq = inverse * inverse
            strength = inverse_sq * inverse
            turning = (product * inverse_sq) * strength
            total[...] += dot(
                jnp.concatenate((pull, pull, swing, swing), 1),
                jnp.concatenate(high_low(strength) + high_low(turning), 0),
                NN,
            )
            return 0

        lax.fori_loop(0, SHARD // CHUNK, step, 0, unroll=UNROLL)
    sums = total[0:8] + total[8:16] + total[16:24]
    place, speed = target[0:3], target[3:6]
    accel = sums[0:3] - place * sums[6:7]
    jerk = sums[3:6] - speed * sums[6:7] + place * sums[7:8]
    spare = rows[pl.ds(7 + where[3], 1), :]
    for member in range(MEMBERS):
        out[member, 0:3, :] = accel
        out[member, 3:6, :] = jerk
        out[member, 6:7, :] = spare
        out[member, 7:8, :] = spare


def correct_kernel(received, out):
    for part in range(2):
        at_member = [PAIRED.index((zh, y, part)) for zh, y, _ in ALONE]
        force = received[at_member[0]]
        for member in at_member[1:]:
            force = force + received[member]
        dt = received[at_member[0], 6:7, :]
        bases = [received[member, 6:7, :] for member in at_member[1:7]]
        accel, jerk = force[0:3], force[3:6]
        half = 0.5 * dt
        step_sq = dt * dt * ONE_TWELFTH
        velocity = jnp.concatenate(bases[3:6], 0) + half * accel - step_sq * jerk
        position = jnp.concatenate(bases[0:3], 0) + half * velocity - step_sq * accel
        at = slice(part * PART, (part + 1) * PART)
        out[0:3, at] = position
        out[3:6, at] = velocity
        out[6:9, at] = accel
        out[9:12, at] = jerk


def local(star_state, star_mass, star_level, active_slots):
    core, helper = lax.axis_index("core"), lax.axis_index("xh")
    y, zh = lax.axis_index("y"), lax.axis_index("zh")
    sender = sender_of(y, zh)
    where = jnp.stack([(y * 2 + zh) * SOURCES, core, helper, sender]).astype(jnp.int32)
    slots = pl.pallas_call(
        slots_kernel,
        out_shape=jax.ShapeDtypeStruct((8, 128), jnp.int32),
        in_specs=[FULL],
        out_specs=FULL,
        compiler_params=PARAMS,
        cost_estimate=LONG,
        name="slots",
    )(active_slots.reshape(8, 128))
    passed = lax.ppermute(slots, ("xh", "xl"), [(x, 3 - x) for x in range(4)])
    anywhere = pl.BlockSpec(memory_space=pl.ANY)
    table = pl.pallas_call(
        table_kernel,
        out_shape=jax.ShapeDtypeStruct((ROWS, SHARD), f32),
        in_specs=[anywhere] * 3,
        out_specs=FULL,
        scratch_shapes=[
            pltpu.VMEM((12, SHARD), f32),
            pltpu.VMEM((1, SHARD), f32),
            pltpu.VMEM((1, SHARD), jnp.int32),
            pltpu.SemaphoreType.DMA((3,)),
        ],
        compiler_params=PARAMS,
        cost_estimate=LONG,
        name="table",
    )(star_state, star_mass.reshape(1, SHARD), star_level.reshape(1, SHARD))
    tables = lax.all_gather(table, "core")
    sent = pl.pallas_call(
        lookup_kernel,
        out_shape=jax.ShapeDtypeStruct((SENDERS, 16, PART), f32),
        in_specs=[SCALARS] + [FULL] * 3,
        out_specs=FULL,
        compiler_params=PARAMS,
        name="lookup",
    )(where, slots, passed, tables)
    alone = exchange_groups(ALONE, [(x,) for x in range(4)])
    received = lax.all_to_all(sent, AXES, 0, 0, axis_index_groups=alone)
    partial = pl.pallas_call(
        force_kernel,
        out_shape=jax.ShapeDtypeStruct((MEMBERS, 8, PART), f32),
        in_specs=[SCALARS] + [FULL] * 2,
        out_specs=FULL,
        scratch_shapes=[
            pltpu.VMEM((32, PART), f32),
            pltpu.VMEM((16, PART), f32),
        ],
        compiler_params=PARAMS,
        name="forces",
    )(where, received, tables)
    paired = exchange_groups(PAIRED, [(x, 3 - x) for x in range(2)])
    shares = lax.all_to_all(partial, AXES, 0, 0, axis_index_groups=paired)
    half_result = pl.pallas_call(
        correct_kernel,
        out_shape=jax.ShapeDtypeStruct((12, HALF), f32),
        in_specs=[FULL],
        out_specs=FULL,
        compiler_params=PARAMS,
        name="corrector",
    )(shares)
    halves = lax.all_gather(half_result, "core")
    result = jnp.concatenate([halves[0], halves[1]], 1)
    return jnp.where((active_slots >= 0)[None, :], result, 0.0)


def solution(mesh):
    split_mesh = Mesh(mesh.devices.reshape(SIZES), AXES)
    return jax.shard_map(
        local,
        mesh=split_mesh,
        in_specs=(P(None, BLK), P(BLK), P(BLK), P(ACT)),
        out_specs=P(None, ACT),
        check_vma=False,
    )
```

```python
import functools

import jax
import jax.numpy as jnp
from jax import lax
from jax.experimental import pallas as pl
from jax.experimental.pallas import tpu as pltpu
from jax.sharding import Mesh, PartitionSpec as P

SOFTENING = 0.0025
STARS = 131072
ONE_THIRD = 1.0 / 3.0
ONE_TWELFTH = 1.0 / 12.0
bf16 = jnp.bfloat16
f32 = jnp.float32
AXES = ("y", "zh", "core", "xh", "xl", "zl")
SIZES = (4, 2, 2, 2, 2, 8)
BLK = ("y", "zh", "core")
ACT = ("xh", "xl", "zl")
SHARD = 8192
ROWS = 15
HALF = 512
PART = 256
SENDERS = 8
MEMBERS = 16
Y_ORDER = (2, 1, 3, 0)
ALONE = [(zh, y, 0) for zh in (1, 0) for y in Y_ORDER]
PAIRED = [(zh, y, role) for role in (1, 0) for zh in (1, 0) for y in Y_ORDER]
CHUNK = 512
UNROLL = 16
SOURCES = 2 * SHARD
FULL = pl.BlockSpec(memory_space=pltpu.VMEM)
SCALARS = pl.BlockSpec(memory_space=pltpu.SMEM)
PARAMS = pltpu.CompilerParams(vmem_limit_bytes=48 * 2**20)
LONG = pl.CostEstimate(flops=10**10, bytes_accessed=2**24, transcendentals=0)
NN = (((1,), (0,)), ((), ()))
TN = (((0,), (0,)), ((), ()))
dot = functools.partial(lax.dot_general, preferred_element_type=f32)


def exchange_groups(order, columns_of):
    return [
        [
            (((y * 2 + zh) * 2 + core) * 4 + columns[role]) * 8 + zl
            for zh, y, role in order
        ]
        for core in range(2)
        for columns in columns_of
        for zl in range(8)
    ]


def rows_of(value):
    return lax.broadcasted_iota(jnp.int32, value.shape, 0)


def split(value):
    high = value.astype(bf16).astype(f32)
    rest = value - high
    middle = rest.astype(bf16).astype(f32)
    return high, middle, rest - middle


def swap_blocks(value):
    row = rows_of(value)
    block = lax.broadcasted_iota(jnp.int32, value.shape, 1) >> 5
    result = jnp.zeros_like(value)
    for shift in range(8):
        moved = pltpu.roll(value, 32 * shift, 1) if shift else value
        kept = jnp.where(block == row, moved, 0.0)
        result = result + (pltpu.roll(kept, 8 - shift, 0) if shift else kept)
    return result


def high_low(value):
    high = value.astype(bf16)
    return high, (value - high.astype(f32)).astype(bf16)


def slots_kernel(slots_in, slots):
    slots[...] = slots_in[...]


def table_kernel(state_in, mass_in, level_in, table, state, mass, level, done):
    copies = [
        pltpu.make_async_copy(source, target, done.at[k])
        for k, (source, target) in enumerate(
            ((state_in, state), (mass_in, mass), (level_in, level))
        )
    ]
    for copy in copies:
        copy.start()
    for copy in copies:
        copy.wait()
    lev = level[...]
    dt = jnp.where(lev == 0, 0.375, jnp.where(lev == 3, 0.0625, 0.125)).astype(f32)
    x, v, a, j = state[0:3], state[3:6], state[6:9], state[9:12]
    place = x + dt * (v + dt * 0.5 * (a + dt * ONE_THIRD * j))
    speed = v + dt * (a + dt * 0.5 * j)
    step_sq = dt * dt * ONE_TWELFTH
    half = 0.5 * dt
    table[0:3, :] = place
    table[3:6, :] = speed
    table[6:7, :] = mass[...]
    table[7:8, :] = dt
    table[8:11, :] = x + half * v + step_sq * a
    table[11:14, :] = v + half * a + step_sq * j
    table[14:15, :] = jnp.sum(place * place, 0, keepdims=True)


def lookup_kernel(where, own_slots, passed_slots, tables, out):
    first, core, helper = where[0], where[1], where[2]
    at = pl.ds(core * 4 + helper * 2, 2)
    index = jnp.where(helper == 0, own_slots[at, :], passed_slots[at, :])
    index = jnp.concatenate((index[0:1], index[1:2]), 1)
    picked = jnp.zeros((16, PART), f32)
    spare = jnp.zeros((16 - ROWS, 128), f32)
    for k in range(2):
        local_index = index - (first + k * SHARD)
        low, high = local_index & 127, local_index >> 7
        low = jnp.broadcast_to(low, (128, PART))
        hit = jnp.where(rows_of(low) == low, 1.0, 0.0).astype(bf16)
        hits = jnp.concatenate((hit, hit, hit), 0)
        high = jnp.broadcast_to(high, (16, PART))
        for block in range(SHARD // 2048):
            tiles = []
            for i in range(block * 16, block * 16 + 16):
                tiles += [tables[k, :, i * 128 : (i + 1) * 128], spare]
            parts = [part.astype(bf16) for part in split(jnp.concatenate(tiles, 0))]
            found = dot(jnp.concatenate(parts, 1), hits, NN)
            for i in range(16):
                picked = jnp.where(high == block * 16 + i, found[16 * i : 16 * i + 16], picked)
    bases = swap_blocks(jnp.where(rows_of(picked[8:16]) < 6, picked[8:16], 0.0))
    for member in range(SENDERS):
        out[member, 0:6, :] = picked[0:6]
        out[member, 6:7, :] = picked[7:8]
        out[member, 7:8, :] = bases[member : member + 1]


def source_features(upper, place_sq):
    row = rows_of(upper)
    speed = pltpu.roll(upper, 5, 0)
    product = 3.0 * jnp.sum(jnp.where(row < 3, upper * speed, 0.0), 0, keepdims=True)
    a, b, c = split(jnp.where(row == 7, 1.0, upper))
    d, e, f = split(jnp.where(row == 6, place_sq, jnp.where(row == 7, product, 0.0)))
    zero = jnp.zeros_like(a)
    features = jnp.concatenate((a, a, a, b, b, c, d, e, f, zero), 0).astype(bf16)
    weight = upper[6:7] * (1.0 / STARS)
    moved = jnp.where(row == 7, 0.0, jnp.where(row == 6, 1.0, upper)) * weight
    placed = pltpu.roll(moved, 3, 0)
    turned = jnp.where(row == 7, weight, jnp.where((row >= 3) & (row < 6), -placed, 0.0))
    pull, swing = [
        jnp.concatenate(split(value) + (zero,), 0).astype(bf16) for value in (moved, turned)
    ]
    return features, pull, swing


def target_features(target):
    row = rows_of(target)
    place = jnp.where(row < 3, target, 0.0)
    speed = pltpu.roll(target, 5, 0)
    place_sq = jnp.sum(place * place, 0, keepdims=True) + SOFTENING
    product = 3.0 * jnp.sum(place * speed, 0, keepdims=True)
    shifted = pltpu.roll(target, 3, 0)
    radius = jnp.where(row == 7, place_sq, -2.0 * place)
    near = jnp.where(
        row == 7,
        product,
        jnp.where(row < 3, -3.0 * speed, jnp.where(row < 6, -3.0 * shifted, 0.0)),
    )
    zero = jnp.zeros_like(target)
    result = []
    for value, own_row in ((radius, 6), (near, 7)):
        a, b, c = split(value)
        one = jnp.where(row == own_row, 1.0, 0.0)
        result.append(
            jnp.concatenate((a, b, c, a, b, a, one, one, one, zero), 0).astype(bf16)
        )
    return result


def force_kernel(received, tables, out, total):
    target = received[0]
    for sender in range(1, SENDERS):
        target = target + received[sender]
    radius_part, near_part = target_features(target)
    total[...] = jnp.zeros_like(total)
    for k in range(2):

        def step(turn, _, k=k):
            at = pl.ds(pl.multiple_of(turn * CHUNK, CHUNK), CHUNK)
            source, pull, swing = source_features(tables[k, 0:8, at], tables[k, 14:15, at])
            radius_sq = dot(source, radius_part, TN)
            product = dot(source, near_part, TN)
            inverse = lax.rsqrt(radius_sq)
            inverse_sq = inverse * inverse
            strength = inverse_sq * inverse
            turning = (product * inverse_sq) * strength
            total[...] += dot(
                jnp.concatenate((pull, pull, swing, swing), 1),
                jnp.concatenate(high_low(strength) + high_low(turning), 0),
                NN,
            )
            return 0

        lax.fori_loop(0, SHARD // CHUNK, step, 0, unroll=UNROLL)
    sums = total[0:8] + total[8:16] + total[16:24]
    place, speed = target[0:3], target[3:6]
    accel = sums[0:3] - place * sums[6:7]
    jerk = sums[3:6] - speed * sums[6:7] + place * sums[7:8]
    for member in range(MEMBERS):
        out[member, 0:3, :] = accel
        out[member, 3:6, :] = jerk
        out[member, 6:7, :] = target[7:8]
        out[member, 7:8, :] = target[6:7]


def correct_kernel(received, out):
    for part in range(2):
        at_member = [PAIRED.index((zh, y, part)) for zh, y, _ in ALONE]
        force = received[at_member[0]]
        for member in at_member[1:]:
            force = force + received[member]
        dt = received[at_member[0], 7:8, :]
        pieces = [received[member, 6:7, :] for member in at_member]
        bases = swap_blocks(jnp.concatenate(pieces, 0))
        accel, jerk = force[0:3], force[3:6]
        half = 0.5 * dt
        step_sq = dt * dt * ONE_TWELFTH
        velocity = bases[3:6] + half * accel - step_sq * jerk
        position = bases[0:3] + half * velocity - step_sq * accel
        at = slice(part * PART, (part + 1) * PART)
        out[0:3, at] = position
        out[3:6, at] = velocity
        out[6:9, at] = accel
        out[9:12, at] = jerk


def local(star_state, star_mass, star_level, active_slots):
    core, helper = lax.axis_index("core"), lax.axis_index("xh")
    y, zh = lax.axis_index("y"), lax.axis_index("zh")
    where = jnp.stack([(y * 2 + zh) * SOURCES, core, helper]).astype(jnp.int32)
    slots = pl.pallas_call(
        slots_kernel,
        out_shape=jax.ShapeDtypeStruct((8, 128), jnp.int32),
        in_specs=[FULL],
        out_specs=FULL,
        compiler_params=PARAMS,
        cost_estimate=LONG,
        name="slots",
    )(active_slots.reshape(8, 128))
    passed = lax.ppermute(slots, ("xh", "xl"), [(x, 3 - x) for x in range(4)])
    anywhere = pl.BlockSpec(memory_space=pl.ANY)
    table = pl.pallas_call(
        table_kernel,
        out_shape=jax.ShapeDtypeStruct((ROWS, SHARD), f32),
        in_specs=[anywhere] * 3,
        out_specs=FULL,
        scratch_shapes=[
            pltpu.VMEM((12, SHARD), f32),
            pltpu.VMEM((1, SHARD), f32),
            pltpu.VMEM((1, SHARD), jnp.int32),
            pltpu.SemaphoreType.DMA((3,)),
        ],
        compiler_params=PARAMS,
        cost_estimate=LONG,
        name="table",
    )(star_state, star_mass.reshape(1, SHARD), star_level.reshape(1, SHARD))
    tables = lax.all_gather(table, "core")
    sent = pl.pallas_call(
        lookup_kernel,
        out_shape=jax.ShapeDtypeStruct((SENDERS, 8, PART), f32),
        in_specs=[SCALARS] + [FULL] * 3,
        out_specs=FULL,
        compiler_params=PARAMS,
        name="lookup",
    )(where, slots, passed, tables)
    alone = exchange_groups(ALONE, [(x,) for x in range(4)])
    received = lax.all_to_all(sent, AXES, 0, 0, axis_index_groups=alone)
    partial = pl.pallas_call(
        force_kernel,
        out_shape=jax.ShapeDtypeStruct((MEMBERS, 8, PART), f32),
        in_specs=[FULL] * 2,
        out_specs=FULL,
        scratch_shapes=[pltpu.VMEM((32, PART), f32)],
        compiler_params=PARAMS,
        name="forces",
    )(received, tables)
    paired = exchange_groups(PAIRED, [(x, 3 - x) for x in range(2)])
    shares = lax.all_to_all(partial, AXES, 0, 0, axis_index_groups=paired)
    half_result = pl.pallas_call(
        correct_kernel,
        out_shape=jax.ShapeDtypeStruct((12, HALF), f32),
        in_specs=[FULL],
        out_specs=FULL,
        compiler_params=PARAMS,
        name="corrector",
    )(shares)
    halves = lax.all_gather(half_result, "core")
    result = jnp.concatenate([halves[0], halves[1]], 1)
    return jnp.where((active_slots >= 0)[None, :], result, 0.0)


def solution(mesh):
    split_mesh = Mesh(mesh.devices.reshape(SIZES), AXES)
    return jax.shard_map(
        local,
        mesh=split_mesh,
        in_specs=(P(None, BLK), P(BLK), P(BLK), P(ACT)),
        out_specs=P(None, ACT),
        check_vma=False,
    )
```

```python
import functools

import jax
import jax.numpy as jnp
from jax import lax
from jax.experimental import pallas as pl
from jax.experimental.pallas import tpu as pltpu
from jax.sharding import Mesh, PartitionSpec as P

SOFTENING = 0.0025
STARS = 131072
ONE_THIRD = 1.0 / 3.0
ONE_TWELFTH = 1.0 / 12.0
bf16 = jnp.bfloat16
f32 = jnp.float32
AXES = ("y", "zh", "core", "xh", "xl", "zl")
SIZES = (4, 2, 2, 2, 2, 8)
BLK = ("y", "zh", "core")
ACT = ("xh", "xl", "zl")
SHARD = 8192
ROWS = 14
HALF = 512
PART = 256
SENDERS = 8
MEMBERS = 16
Y_ORDER = (2, 1, 3, 0)
ALONE = [(zh, y, 0) for zh in (1, 0) for y in Y_ORDER]
PAIRED = [(zh, y, role) for role in (1, 0) for zh in (1, 0) for y in Y_ORDER]
CHUNK = 512
UNROLL = 16
SOURCES = 2 * SHARD
FULL = pl.BlockSpec(memory_space=pltpu.VMEM)
SCALARS = pl.BlockSpec(memory_space=pltpu.SMEM)
PARAMS = pltpu.CompilerParams(vmem_limit_bytes=48 * 2**20)
LONG = pl.CostEstimate(flops=10**10, bytes_accessed=2**24, transcendentals=0)
NN = (((1,), (0,)), ((), ()))
TN = (((0,), (0,)), ((), ()))
dot = functools.partial(lax.dot_general, preferred_element_type=f32)


def exchange_groups(order, columns_of):
    return [
        [
            (((y * 2 + zh) * 2 + core) * 4 + columns[role]) * 8 + zl
            for zh, y, role in order
        ]
        for core in range(2)
        for columns in columns_of
        for zl in range(8)
    ]


def rows_of(value):
    return lax.broadcasted_iota(jnp.int32, value.shape, 0)


def split(value):
    high = value.astype(bf16).astype(f32)
    rest = value - high
    middle = rest.astype(bf16).astype(f32)
    return high, middle, rest - middle


def swap_blocks(value):
    row = rows_of(value)
    block = lax.broadcasted_iota(jnp.int32, value.shape, 1) >> 5
    result = jnp.zeros_like(value)
    for shift in range(8):
        moved = pltpu.roll(value, 32 * shift, 1) if shift else value
        kept = jnp.where(block == row, moved, 0.0)
        result = result + (pltpu.roll(kept, 8 - shift, 0) if shift else kept)
    return result


def high_low(value):
    high = value.astype(bf16)
    return high, (value - high.astype(f32)).astype(bf16)


def slots_kernel(slots_in, slots):
    slots[...] = slots_in[...]


def table_kernel(state_in, mass_in, level_in, table, state, mass, level, done):
    copies = [
        pltpu.make_async_copy(source, target, done.at[k])
        for k, (source, target) in enumerate(
            ((state_in, state), (mass_in, mass), (level_in, level))
        )
    ]
    for copy in copies:
        copy.start()
    for copy in copies:
        copy.wait()
    lev = level[...]
    dt = jnp.where(lev == 0, 0.375, jnp.where(lev == 3, 0.0625, 0.125)).astype(f32)
    x, v, a, j = state[0:3], state[3:6], state[6:9], state[9:12]
    place = x + dt * (v + dt * 0.5 * (a + dt * ONE_THIRD * j))
    speed = v + dt * (a + dt * 0.5 * j)
    step_sq = dt * dt * ONE_TWELFTH
    half = 0.5 * dt
    table[0:3, :] = place
    table[3:6, :] = speed
    table[6:7, :] = mass[...]
    table[7:8, :] = dt
    table[8:11, :] = x + half * v + step_sq * a
    table[11:14, :] = v + half * a + step_sq * j


def lookup_kernel(where, own_slots, passed_slots, tables, out):
    first, core, helper = where[0], where[1], where[2]
    at = pl.ds(core * 4 + helper * 2, 2)
    index = jnp.where(helper == 0, own_slots[at, :], passed_slots[at, :])
    index = jnp.concatenate((index[0:1], index[1:2]), 1)
    picked = jnp.zeros((16, PART), f32)
    spare = jnp.zeros((16 - ROWS, 128), f32)
    for k in range(2):
        local_index = index - (first + k * SHARD)
        low, high = local_index & 127, local_index >> 7
        low = jnp.broadcast_to(low, (128, PART))
        hit = jnp.where(rows_of(low) == low, 1.0, 0.0).astype(bf16)
        hits = jnp.concatenate((hit, hit, hit), 0)
        high = jnp.broadcast_to(high, (16, PART))
        for block in range(SHARD // 2048):
            tiles = []
            for i in range(block * 16, block * 16 + 16):
                tiles += [tables[k, :, i * 128 : (i + 1) * 128], spare]
            parts = [part.astype(bf16) for part in split(jnp.concatenate(tiles, 0))]
            found = dot(jnp.concatenate(parts, 1), hits, NN)
            for i in range(16):
                picked = jnp.where(high == block * 16 + i, found[16 * i : 16 * i + 16], picked)
    bases = swap_blocks(jnp.where(rows_of(picked[8:16]) < 6, picked[8:16], 0.0))
    for member in range(SENDERS):
        out[member, 0:6, :] = picked[0:6]
        out[member, 6:7, :] = picked[7:8]
        out[member, 7:8, :] = bases[member : member + 1]


def source_features(upper):
    row = rows_of(upper)
    place_sq = jnp.sum(jnp.where(row < 3, upper * upper, 0.0), 0, keepdims=True)
    speed = pltpu.roll(upper, 5, 0)
    product = 3.0 * jnp.sum(jnp.where(row < 3, upper * speed, 0.0), 0, keepdims=True)
    a, b, c = split(jnp.where(row == 7, 1.0, upper))
    d, e, f = split(jnp.where(row == 6, place_sq, jnp.where(row == 7, product, 0.0)))
    zero = jnp.zeros_like(a)
    features = jnp.concatenate((a, a, a, b, b, c, d, e, f, zero), 0).astype(bf16)
    weight = upper[6:7] * (1.0 / STARS)
    moved = jnp.where(row == 7, 0.0, jnp.where(row == 6, 1.0, upper)) * weight
    placed = pltpu.roll(moved, 3, 0)
    turned = jnp.where(row == 7, weight, jnp.where((row >= 3) & (row < 6), -placed, 0.0))
    pull, swing = [
        jnp.concatenate(split(value) + (zero,), 0).astype(bf16) for value in (moved, turned)
    ]
    return features, pull, swing


def target_features(target):
    row = rows_of(target)
    place = jnp.where(row < 3, target, 0.0)
    speed = pltpu.roll(target, 5, 0)
    place_sq = jnp.sum(place * place, 0, keepdims=True) + SOFTENING
    product = 3.0 * jnp.sum(place * speed, 0, keepdims=True)
    shifted = pltpu.roll(target, 3, 0)
    radius = jnp.where(row == 7, place_sq, -2.0 * place)
    near = jnp.where(
        row == 7,
        product,
        jnp.where(row < 3, -3.0 * speed, jnp.where(row < 6, -3.0 * shifted, 0.0)),
    )
    zero = jnp.zeros_like(target)
    result = []
    for value, own_row in ((radius, 6), (near, 7)):
        a, b, c = split(value)
        one = jnp.where(row == own_row, 1.0, 0.0)
        result.append(
            jnp.concatenate((a, b, c, a, b, a, one, one, one, zero), 0).astype(bf16)
        )
    return result


def force_kernel(received, tables, out, total):
    target = received[0]
    for sender in range(1, SENDERS):
        target = target + received[sender]
    centre = sum(jnp.sum(tables[k, 0:8, :], 1, keepdims=True) for k in range(2))
    centre = jnp.where(rows_of(centre) < 6, centre * (1.0 / SOURCES), 0.0)
    target = target - centre
    radius_part, near_part = target_features(target)
    total[...] = jnp.zeros_like(total)
    for k in range(2):

        def step(turn, _, k=k):
            at = pl.ds(pl.multiple_of(turn * CHUNK, CHUNK), CHUNK)
            source, pull, swing = source_features(tables[k, 0:8, at] - centre)
            radius_sq = dot(source, radius_part, TN)
            product = dot(source, near_part, TN)
            inverse = lax.rsqrt(radius_sq)
            inverse_sq = inverse * inverse
            strength = inverse_sq * inverse
            turning = (product * inverse_sq) * strength
            total[...] += dot(
                jnp.concatenate((pull, pull, swing, swing), 1),
                jnp.concatenate(high_low(strength) + high_low(turning), 0),
                NN,
            )
            return 0

        lax.fori_loop(0, SHARD // CHUNK, step, 0, unroll=UNROLL)
    sums = total[0:8] + total[8:16] + total[16:24]
    place, speed = target[0:3], target[3:6]
    accel = sums[0:3] - place * sums[6:7]
    jerk = sums[3:6] - speed * sums[6:7] + place * sums[7:8]
    for member in range(MEMBERS):
        out[member, 0:3, :] = accel
        out[member, 3:6, :] = jerk
        out[member, 6:7, :] = target[7:8]
        out[member, 7:8, :] = target[6:7]


def correct_kernel(received, out):
    for part in range(2):
        at_member = [PAIRED.index((zh, y, part)) for zh, y, _ in ALONE]
        force = received[at_member[0]]
        for member in at_member[1:]:
            force = force + received[member]
        dt = received[at_member[0], 7:8, :]
        pieces = [received[member, 6:7, :] for member in at_member]
        bases = swap_blocks(jnp.concatenate(pieces, 0))
        accel, jerk = force[0:3], force[3:6]
        half = 0.5 * dt
        step_sq = dt * dt * ONE_TWELFTH
        velocity = bases[3:6] + half * accel - step_sq * jerk
        position = bases[0:3] + half * velocity - step_sq * accel
        at = slice(part * PART, (part + 1) * PART)
        out[0:3, at] = position
        out[3:6, at] = velocity
        out[6:9, at] = accel
        out[9:12, at] = jerk


def local(star_state, star_mass, star_level, active_slots):
    core, helper = lax.axis_index("core"), lax.axis_index("xh")
    y, zh = lax.axis_index("y"), lax.axis_index("zh")
    where = jnp.stack([(y * 2 + zh) * SOURCES, core, helper]).astype(jnp.int32)
    slots = pl.pallas_call(
        slots_kernel,
        out_shape=jax.ShapeDtypeStruct((8, 128), jnp.int32),
        in_specs=[FULL],
        out_specs=FULL,
        compiler_params=PARAMS,
        cost_estimate=LONG,
        name="slots",
    )(active_slots.reshape(8, 128))
    passed = lax.ppermute(slots, ("xh", "xl"), [(x, 3 - x) for x in range(4)])
    anywhere = pl.BlockSpec(memory_space=pl.ANY)
    table = pl.pallas_call(
        table_kernel,
        out_shape=jax.ShapeDtypeStruct((ROWS, SHARD), f32),
        in_specs=[anywhere] * 3,
        out_specs=FULL,
        scratch_shapes=[
            pltpu.VMEM((12, SHARD), f32),
            pltpu.VMEM((1, SHARD), f32),
            pltpu.VMEM((1, SHARD), jnp.int32),
            pltpu.SemaphoreType.DMA((3,)),
        ],
        compiler_params=PARAMS,
        cost_estimate=LONG,
        name="table",
    )(star_state, star_mass.reshape(1, SHARD), star_level.reshape(1, SHARD))
    tables = lax.all_gather(table, "core")
    sent = pl.pallas_call(
        lookup_kernel,
        out_shape=jax.ShapeDtypeStruct((SENDERS, 8, PART), f32),
        in_specs=[SCALARS] + [FULL] * 3,
        out_specs=FULL,
        compiler_params=PARAMS,
        name="lookup",
    )(where, slots, passed, tables)
    alone = exchange_groups(ALONE, [(x,) for x in range(4)])
    received = lax.all_to_all(sent, AXES, 0, 0, axis_index_groups=alone)
    partial = pl.pallas_call(
        force_kernel,
        out_shape=jax.ShapeDtypeStruct((MEMBERS, 8, PART), f32),
        in_specs=[FULL] * 2,
        out_specs=FULL,
        scratch_shapes=[pltpu.VMEM((32, PART), f32)],
        compiler_params=PARAMS,
        name="forces",
    )(received, tables)
    paired = exchange_groups(PAIRED, [(x, 3 - x) for x in range(2)])
    shares = lax.all_to_all(partial, AXES, 0, 0, axis_index_groups=paired)
    half_result = pl.pallas_call(
        correct_kernel,
        out_shape=jax.ShapeDtypeStruct((12, HALF), f32),
        in_specs=[FULL],
        out_specs=FULL,
        compiler_params=PARAMS,
        name="corrector",
    )(shares)
    halves = lax.all_gather(half_result, "core")
    result = jnp.concatenate([halves[0], halves[1]], 1)
    return jnp.where((active_slots >= 0)[None, :], result, 0.0)


def solution(mesh):
    split_mesh = Mesh(mesh.devices.reshape(SIZES), AXES)
    return jax.shard_map(
        local,
        mesh=split_mesh,
        in_specs=(P(None, BLK), P(BLK), P(BLK), P(ACT)),
        out_specs=P(None, ACT),
        check_vma=False,
    )
```

```python
import functools

import jax
import jax.numpy as jnp
from jax import lax
from jax.experimental import pallas as pl
from jax.experimental.pallas import tpu as pltpu
from jax.sharding import Mesh, PartitionSpec as P

SOFTENING = 0.0025
STARS = 131072
ONE_THIRD = 1.0 / 3.0
ONE_TWELFTH = 1.0 / 12.0
bf16 = jnp.bfloat16
f32 = jnp.float32
AXES = ("y", "zh", "core", "xh", "xl", "zl")
SIZES = (4, 2, 2, 2, 2, 8)
BLK = ("y", "zh", "core")
ACT = ("xh", "xl", "zl")
SHARD = 8192
ROWS = 14
SAMPLE = 1024
HALF = 512
PART = 256
SENDERS = 8
MEMBERS = 16
Y_ORDER = (2, 1, 3, 0)
ALONE = [(zh, y, 0) for zh in (1, 0) for y in Y_ORDER]
PAIRED = [(zh, y, role) for role in (1, 0) for zh in (1, 0) for y in Y_ORDER]
CHUNK = 512
UNROLL = 16
SOURCES = 2 * SHARD
FULL = pl.BlockSpec(memory_space=pltpu.VMEM)
SCALARS = pl.BlockSpec(memory_space=pltpu.SMEM)
PARAMS = pltpu.CompilerParams(vmem_limit_bytes=48 * 2**20)
LONG = pl.CostEstimate(flops=10**10, bytes_accessed=2**24, transcendentals=0)
NN = (((1,), (0,)), ((), ()))
TN = (((0,), (0,)), ((), ()))
dot = functools.partial(lax.dot_general, preferred_element_type=f32)


def exchange_groups(order, columns_of):
    return [
        [
            (((y * 2 + zh) * 2 + core) * 4 + columns[role]) * 8 + zl
            for zh, y, role in order
        ]
        for core in range(2)
        for columns in columns_of
        for zl in range(8)
    ]


def rows_of(value):
    return lax.broadcasted_iota(jnp.int32, value.shape, 0)


def split(value):
    high = value.astype(bf16).astype(f32)
    rest = value - high
    middle = rest.astype(bf16).astype(f32)
    return high, middle, rest - middle


def swap_blocks(value):
    row = rows_of(value)
    block = lax.broadcasted_iota(jnp.int32, value.shape, 1) >> 5
    result = jnp.zeros_like(value)
    for shift in range(8):
        moved = pltpu.roll(value, 32 * shift, 1) if shift else value
        kept = jnp.where(block == row, moved, 0.0)
        result = result + (pltpu.roll(kept, 8 - shift, 0) if shift else kept)
    return result


def high_low(value):
    high = value.astype(bf16)
    return high, (value - high.astype(f32)).astype(bf16)


def slots_kernel(slots_in, slots):
    slots[...] = slots_in[...]


def table_kernel(state_in, mass_in, level_in, table, state, mass, level, done):
    copies = [
        pltpu.make_async_copy(source, target, done.at[k])
        for k, (source, target) in enumerate(
            ((state_in, state), (mass_in, mass), (level_in, level))
        )
    ]
    for copy in copies:
        copy.start()
    for copy in copies:
        copy.wait()
    lev = level[...]
    dt = jnp.where(lev == 0, 0.375, jnp.where(lev == 3, 0.0625, 0.125)).astype(f32)
    x, v, a, j = state[0:3], state[3:6], state[6:9], state[9:12]
    place = x + dt * (v + dt * 0.5 * (a + dt * ONE_THIRD * j))
    speed = v + dt * (a + dt * 0.5 * j)
    step_sq = dt * dt * ONE_TWELFTH
    half = 0.5 * dt
    table[0:3, :] = place
    table[3:6, :] = speed
    table[6:7, :] = mass[...]
    table[7:8, :] = dt
    table[8:11, :] = x + half * v + step_sq * a
    table[11:14, :] = v + half * a + step_sq * j


def lookup_kernel(where, own_slots, passed_slots, tables, out):
    first, core, helper = where[0], where[1], where[2]
    at = pl.ds(core * 4 + helper * 2, 2)
    index = jnp.where(helper == 0, own_slots[at, :], passed_slots[at, :])
    index = jnp.concatenate((index[0:1], index[1:2]), 1)
    picked = jnp.zeros((16, PART), f32)
    spare = jnp.zeros((16 - ROWS, 128), f32)
    for k in range(2):
        local_index = index - (first + k * SHARD)
        low, high = local_index & 127, local_index >> 7
        low = jnp.broadcast_to(low, (128, PART))
        hit = jnp.where(rows_of(low) == low, 1.0, 0.0).astype(bf16)
        hits = jnp.concatenate((hit, hit, hit), 0)
        high = jnp.broadcast_to(high, (16, PART))
        for block in range(SHARD // 2048):
            tiles = []
            for i in range(block * 16, block * 16 + 16):
                tiles += [tables[k, :, i * 128 : (i + 1) * 128], spare]
            parts = [part.astype(bf16) for part in split(jnp.concatenate(tiles, 0))]
            found = dot(jnp.concatenate(parts, 1), hits, NN)
            for i in range(16):
                picked = jnp.where(high == block * 16 + i, found[16 * i : 16 * i + 16], picked)
    bases = swap_blocks(jnp.where(rows_of(picked[8:16]) < 6, picked[8:16], 0.0))
    for member in range(SENDERS):
        out[member, 0:6, :] = picked[0:6]
        out[member, 6:7, :] = picked[7:8]
        out[member, 7:8, :] = bases[member : member + 1]


def source_features(upper):
    row = rows_of(upper)
    place_sq = jnp.sum(jnp.where(row < 3, upper * upper, 0.0), 0, keepdims=True)
    speed = pltpu.roll(upper, 5, 0)
    product = 3.0 * jnp.sum(jnp.where(row < 3, upper * speed, 0.0), 0, keepdims=True)
    a, b, c = split(jnp.where(row == 7, 1.0, upper))
    d, e, f = split(jnp.where(row == 6, place_sq, jnp.where(row == 7, product, 0.0)))
    zero = jnp.zeros_like(a)
    features = jnp.concatenate((a, a, a, b, b, c, d, e, f, zero), 0).astype(bf16)
    weight = upper[6:7] * (1.0 / STARS)
    moved = jnp.where(row == 7, 0.0, jnp.where(row == 6, 1.0, upper)) * weight
    placed = pltpu.roll(moved, 3, 0)
    turned = jnp.where(row == 7, weight, jnp.where((row >= 3) & (row < 6), -placed, 0.0))
    pull, swing = [
        jnp.concatenate(split(value) + (zero,), 0).astype(bf16) for value in (moved, turned)
    ]
    return features, pull, swing


def target_features(target):
    row = rows_of(target)
    place = jnp.where(row < 3, target, 0.0)
    speed = pltpu.roll(target, 5, 0)
    place_sq = jnp.sum(place * place, 0, keepdims=True) + SOFTENING
    product = 3.0 * jnp.sum(place * speed, 0, keepdims=True)
    shifted = pltpu.roll(target, 3, 0)
    radius = jnp.where(row == 7, place_sq, -2.0 * place)
    near = jnp.where(
        row == 7,
        product,
        jnp.where(row < 3, -3.0 * speed, jnp.where(row < 6, -3.0 * shifted, 0.0)),
    )
    zero = jnp.zeros_like(target)
    result = []
    for value, own_row in ((radius, 6), (near, 7)):
        a, b, c = split(value)
        one = jnp.where(row == own_row, 1.0, 0.0)
        result.append(
            jnp.concatenate((a, b, c, a, b, a, one, one, one, zero), 0).astype(bf16)
        )
    return result


def force_kernel(received, tables, out, total):
    target = received[0]
    for sender in range(1, SENDERS):
        target = target + received[sender]
    centre = jnp.sum(tables[0, 0:8, 0:SAMPLE], 1, keepdims=True)
    centre = jnp.where(rows_of(centre) < 6, centre * (1.0 / SAMPLE), 0.0)
    target = target - centre
    radius_part, near_part = target_features(target)
    total[...] = jnp.zeros_like(total)
    for k in range(2):

        def step(turn, _, k=k):
            at = pl.ds(pl.multiple_of(turn * CHUNK, CHUNK), CHUNK)
            source, pull, swing = source_features(tables[k, 0:8, at] - centre)
            radius_sq = dot(source, radius_part, TN)
            product = dot(source, near_part, TN)
            inverse = lax.rsqrt(radius_sq)
            inverse_sq = inverse * inverse
            strength = inverse_sq * inverse
            turning = (product * inverse_sq) * strength
            total[...] += dot(
                jnp.concatenate((pull, pull, swing, swing), 1),
                jnp.concatenate(high_low(strength) + high_low(turning), 0),
                NN,
            )
            return 0

        lax.fori_loop(0, SHARD // CHUNK, step, 0, unroll=UNROLL)
    sums = total[0:8] + total[8:16] + total[16:24]
    place, speed = target[0:3], target[3:6]
    accel = sums[0:3] - place * sums[6:7]
    jerk = sums[3:6] - speed * sums[6:7] + place * sums[7:8]
    for member in range(MEMBERS):
        out[member, 0:3, :] = accel
        out[member, 3:6, :] = jerk
        out[member, 6:7, :] = target[7:8]
        out[member, 7:8, :] = target[6:7]


def correct_kernel(received, out):
    for part in range(2):
        at_member = [PAIRED.index((zh, y, part)) for zh, y, _ in ALONE]
        force = received[at_member[0]]
        for member in at_member[1:]:
            force = force + received[member]
        dt = received[at_member[0], 7:8, :]
        pieces = [received[member, 6:7, :] for member in at_member]
        bases = swap_blocks(jnp.concatenate(pieces, 0))
        accel, jerk = force[0:3], force[3:6]
        half = 0.5 * dt
        step_sq = dt * dt * ONE_TWELFTH
        velocity = bases[3:6] + half * accel - step_sq * jerk
        position = bases[0:3] + half * velocity - step_sq * accel
        at = slice(part * PART, (part + 1) * PART)
        out[0:3, at] = position
        out[3:6, at] = velocity
        out[6:9, at] = accel
        out[9:12, at] = jerk


def local(star_state, star_mass, star_level, active_slots):
    core, helper = lax.axis_index("core"), lax.axis_index("xh")
    y, zh = lax.axis_index("y"), lax.axis_index("zh")
    where = jnp.stack([(y * 2 + zh) * SOURCES, core, helper]).astype(jnp.int32)
    slots = pl.pallas_call(
        slots_kernel,
        out_shape=jax.ShapeDtypeStruct((8, 128), jnp.int32),
        in_specs=[FULL],
        out_specs=FULL,
        compiler_params=PARAMS,
        cost_estimate=LONG,
        name="slots",
    )(active_slots.reshape(8, 128))
    passed = lax.ppermute(slots, ("xh", "xl"), [(x, 3 - x) for x in range(4)])
    anywhere = pl.BlockSpec(memory_space=pl.ANY)
    table = pl.pallas_call(
        table_kernel,
        out_shape=jax.ShapeDtypeStruct((ROWS, SHARD), f32),
        in_specs=[anywhere] * 3,
        out_specs=FULL,
        scratch_shapes=[
            pltpu.VMEM((12, SHARD), f32),
            pltpu.VMEM((1, SHARD), f32),
            pltpu.VMEM((1, SHARD), jnp.int32),
            pltpu.SemaphoreType.DMA((3,)),
        ],
        compiler_params=PARAMS,
        cost_estimate=LONG,
        name="table",
    )(star_state, star_mass.reshape(1, SHARD), star_level.reshape(1, SHARD))
    tables = lax.all_gather(table, "core")
    sent = pl.pallas_call(
        lookup_kernel,
        out_shape=jax.ShapeDtypeStruct((SENDERS, 8, PART), f32),
        in_specs=[SCALARS] + [FULL] * 3,
        out_specs=FULL,
        compiler_params=PARAMS,
        name="lookup",
    )(where, slots, passed, tables)
    alone = exchange_groups(ALONE, [(x,) for x in range(4)])
    received = lax.all_to_all(sent, AXES, 0, 0, axis_index_groups=alone)
    partial = pl.pallas_call(
        force_kernel,
        out_shape=jax.ShapeDtypeStruct((MEMBERS, 8, PART), f32),
        in_specs=[FULL] * 2,
        out_specs=FULL,
        scratch_shapes=[pltpu.VMEM((32, PART), f32)],
        compiler_params=PARAMS,
        name="forces",
    )(received, tables)
    paired = exchange_groups(PAIRED, [(x, 3 - x) for x in range(2)])
    shares = lax.all_to_all(partial, AXES, 0, 0, axis_index_groups=paired)
    half_result = pl.pallas_call(
        correct_kernel,
        out_shape=jax.ShapeDtypeStruct((12, HALF), f32),
        in_specs=[FULL],
        out_specs=FULL,
        compiler_params=PARAMS,
        name="corrector",
    )(shares)
    halves = lax.all_gather(half_result, "core")
    result = jnp.concatenate([halves[0], halves[1]], 1)
    return jnp.where((active_slots >= 0)[None, :], result, 0.0)


def solution(mesh):
    split_mesh = Mesh(mesh.devices.reshape(SIZES), AXES)
    return jax.shard_map(
        local,
        mesh=split_mesh,
        in_specs=(P(None, BLK), P(BLK), P(BLK), P(ACT)),
        out_specs=P(None, ACT),
        check_vma=False,
    )
```

```python
import functools

import jax
import jax.numpy as jnp
from jax import lax
from jax.experimental import pallas as pl
from jax.experimental.pallas import tpu as pltpu
from jax.sharding import Mesh, PartitionSpec as P

SOFTENING = 0.0025
STARS = 131072
ONE_THIRD = 1.0 / 3.0
ONE_TWELFTH = 1.0 / 12.0
bf16 = jnp.bfloat16
f32 = jnp.float32
AXES = ("y", "zh", "core", "xh", "xl", "zl")
SIZES = (4, 2, 2, 2, 2, 8)
BLK = ("y", "zh", "core")
ACT = ("xh", "xl", "zl")
SHARD = 8192
ROWS = 14
SAMPLE = 128
HALF = 512
PART = 256
SENDERS = 8
MEMBERS = 16
Y_ORDER = (2, 1, 3, 0)
ALONE = [(zh, y, 0) for zh in (1, 0) for y in Y_ORDER]
PAIRED = [(zh, y, role) for role in (1, 0) for zh in (1, 0) for y in Y_ORDER]
CHUNK = 256
UNROLL = 32
SOURCES = 2 * SHARD
FULL = pl.BlockSpec(memory_space=pltpu.VMEM)
SCALARS = pl.BlockSpec(memory_space=pltpu.SMEM)
PARAMS = pltpu.CompilerParams(vmem_limit_bytes=48 * 2**20)
LONG = pl.CostEstimate(flops=10**10, bytes_accessed=2**24, transcendentals=0)
NN = (((1,), (0,)), ((), ()))
TN = (((0,), (0,)), ((), ()))
dot = functools.partial(lax.dot_general, preferred_element_type=f32)


def exchange_groups(order, columns_of):
    return [
        [
            (((y * 2 + zh) * 2 + core) * 4 + columns[role]) * 8 + zl
            for zh, y, role in order
        ]
        for core in range(2)
        for columns in columns_of
        for zl in range(8)
    ]


def rows_of(value):
    return lax.broadcasted_iota(jnp.int32, value.shape, 0)


def split(value):
    high = value.astype(bf16).astype(f32)
    rest = value - high
    middle = rest.astype(bf16).astype(f32)
    return high, middle, rest - middle


def swap_blocks(value):
    row = rows_of(value)
    block = lax.broadcasted_iota(jnp.int32, value.shape, 1) >> 5
    result = jnp.zeros_like(value)
    for shift in range(8):
        moved = pltpu.roll(value, 32 * shift, 1) if shift else value
        kept = jnp.where(block == row, moved, 0.0)
        result = result + (pltpu.roll(kept, 8 - shift, 0) if shift else kept)
    return result


def high_low(value):
    high = value.astype(bf16)
    return high, (value - high.astype(f32)).astype(bf16)


def slots_kernel(slots_in, slots):
    slots[...] = slots_in[...]


def table_kernel(state_in, mass_in, level_in, table, state, mass, level, done):
    copies = [
        pltpu.make_async_copy(source, target, done.at[k])
        for k, (source, target) in enumerate(
            ((state_in, state), (mass_in, mass), (level_in, level))
        )
    ]
    for copy in copies:
        copy.start()
    for copy in copies:
        copy.wait()
    lev = level[...]
    dt = jnp.where(lev == 0, 0.375, jnp.where(lev == 3, 0.0625, 0.125)).astype(f32)
    x, v, a, j = state[0:3], state[3:6], state[6:9], state[9:12]
    place = x + dt * (v + dt * 0.5 * (a + dt * ONE_THIRD * j))
    speed = v + dt * (a + dt * 0.5 * j)
    step_sq = dt * dt * ONE_TWELFTH
    half = 0.5 * dt
    table[0:3, :] = place
    table[3:6, :] = speed
    table[6:7, :] = mass[...]
    table[7:8, :] = dt
    table[8:11, :] = x + half * v + step_sq * a
    table[11:14, :] = v + half * a + step_sq * j


def lookup_kernel(where, own_slots, passed_slots, tables, out):
    first, core, helper = where[0], where[1], where[2]
    at = pl.ds(core * 4 + helper * 2, 2)
    index = jnp.where(helper == 0, own_slots[at, :], passed_slots[at, :])
    index = jnp.concatenate((index[0:1], index[1:2]), 1)
    picked = jnp.zeros((16, PART), f32)
    spare = jnp.zeros((16 - ROWS, 128), f32)
    for k in range(2):
        local_index = index - (first + k * SHARD)
        low, high = local_index & 127, local_index >> 7
        low = jnp.broadcast_to(low, (128, PART))
        hit = jnp.where(rows_of(low) == low, 1.0, 0.0).astype(bf16)
        hits = jnp.concatenate((hit, hit, hit), 0)
        high = jnp.broadcast_to(high, (16, PART))
        for block in range(SHARD // 2048):
            tiles = []
            for i in range(block * 16, block * 16 + 16):
                tiles += [tables[k, :, i * 128 : (i + 1) * 128], spare]
            parts = [part.astype(bf16) for part in split(jnp.concatenate(tiles, 0))]
            found = dot(jnp.concatenate(parts, 1), hits, NN)
            for i in range(16):
                picked = jnp.where(high == block * 16 + i, found[16 * i : 16 * i + 16], picked)
    bases = swap_blocks(jnp.where(rows_of(picked[8:16]) < 6, picked[8:16], 0.0))
    for member in range(SENDERS):
        out[member, 0:6, :] = picked[0:6]
        out[member, 6:7, :] = picked[7:8]
        out[member, 7:8, :] = bases[member : member + 1]


def source_features(upper):
    row = rows_of(upper)
    place_sq = jnp.sum(jnp.where(row < 3, upper * upper, 0.0), 0, keepdims=True)
    speed = pltpu.roll(upper, 5, 0)
    product = 3.0 * jnp.sum(jnp.where(row < 3, upper * speed, 0.0), 0, keepdims=True)
    a, b, c = split(jnp.where(row == 7, 1.0, upper))
    d, e, f = split(jnp.where(row == 6, place_sq, jnp.where(row == 7, product, 0.0)))
    zero = jnp.zeros_like(a)
    features = jnp.concatenate((a, a, a, b, b, c, d, e, f, zero), 0).astype(bf16)
    weight = upper[6:7] * (1.0 / STARS)
    moved = jnp.where(row == 7, 0.0, jnp.where(row == 6, 1.0, upper)) * weight
    placed = pltpu.roll(moved, 3, 0)
    turned = jnp.where(row == 7, weight, jnp.where((row >= 3) & (row < 6), -placed, 0.0))
    pull, swing = [
        jnp.concatenate(split(value) + (zero,), 0).astype(bf16) for value in (moved, turned)
    ]
    return features, pull, swing


def target_features(target):
    row = rows_of(target)
    place = jnp.where(row < 3, target, 0.0)
    speed = pltpu.roll(target, 5, 0)
    place_sq = jnp.sum(place * place, 0, keepdims=True) + SOFTENING
    product = 3.0 * jnp.sum(place * speed, 0, keepdims=True)
    shifted = pltpu.roll(target, 3, 0)
    radius = jnp.where(row == 7, place_sq, -2.0 * place)
    near = jnp.where(
        row == 7,
        product,
        jnp.where(row < 3, -3.0 * speed, jnp.where(row < 6, -3.0 * shifted, 0.0)),
    )
    zero = jnp.zeros_like(target)
    result = []
    for value, own_row in ((radius, 6), (near, 7)):
        a, b, c = split(value)
        one = jnp.where(row == own_row, 1.0, 0.0)
        result.append(
            jnp.concatenate((a, b, c, a, b, a, one, one, one, zero), 0).astype(bf16)
        )
    return result


def force_kernel(received, tables, out, total):
    target = received[0]
    for sender in range(1, SENDERS):
        target = target + received[sender]
    centre = jnp.sum(tables[0, 0:8, 0:SAMPLE], 1, keepdims=True)
    centre = jnp.where(rows_of(centre) < 6, centre * (1.0 / SAMPLE), 0.0)
    target = target - centre
    radius_part, near_part = target_features(target)
    total[...] = jnp.zeros_like(total)
    for k in range(2):

        def step(turn, _, k=k):
            at = pl.ds(pl.multiple_of(turn * CHUNK, CHUNK), CHUNK)
            source, pull, swing = source_features(tables[k, 0:8, at] - centre)
            radius_sq = dot(source, radius_part, TN)
            product = dot(source, near_part, TN)
            inverse = lax.rsqrt(radius_sq)
            inverse_sq = inverse * inverse
            strength = inverse_sq * inverse
            turning = (product * inverse_sq) * strength
            total[...] += dot(
                jnp.concatenate((pull, pull, swing, swing), 1),
                jnp.concatenate(high_low(strength) + high_low(turning), 0),
                NN,
            )
            return 0

        lax.fori_loop(0, SHARD // CHUNK, step, 0, unroll=UNROLL)
    sums = total[0:8] + total[8:16] + total[16:24]
    place, speed = target[0:3], target[3:6]
    accel = sums[0:3] - place * sums[6:7]
    jerk = sums[3:6] - speed * sums[6:7] + place * sums[7:8]
    for member in range(MEMBERS):
        out[member, 0:3, :] = accel
        out[member, 3:6, :] = jerk
        out[member, 6:7, :] = target[7:8]
        out[member, 7:8, :] = target[6:7]


def correct_kernel(received, out):
    for part in range(2):
        at_member = [PAIRED.index((zh, y, part)) for zh, y, _ in ALONE]
        force = received[at_member[0]]
        for member in at_member[1:]:
            force = force + received[member]
        dt = received[at_member[0], 7:8, :]
        pieces = [received[member, 6:7, :] for member in at_member]
        bases = swap_blocks(jnp.concatenate(pieces, 0))
        accel, jerk = force[0:3], force[3:6]
        half = 0.5 * dt
        step_sq = dt * dt * ONE_TWELFTH
        velocity = bases[3:6] + half * accel - step_sq * jerk
        position = bases[0:3] + half * velocity - step_sq * accel
        at = slice(part * PART, (part + 1) * PART)
        out[0:3, at] = position
        out[3:6, at] = velocity
        out[6:9, at] = accel
        out[9:12, at] = jerk


def local(star_state, star_mass, star_level, active_slots):
    core, helper = lax.axis_index("core"), lax.axis_index("xh")
    y, zh = lax.axis_index("y"), lax.axis_index("zh")
    where = jnp.stack([(y * 2 + zh) * SOURCES, core, helper]).astype(jnp.int32)
    slots = pl.pallas_call(
        slots_kernel,
        out_shape=jax.ShapeDtypeStruct((8, 128), jnp.int32),
        in_specs=[FULL],
        out_specs=FULL,
        compiler_params=PARAMS,
        cost_estimate=LONG,
        name="slots",
    )(active_slots.reshape(8, 128))
    passed = lax.ppermute(slots, ("xh", "xl"), [(x, 3 - x) for x in range(4)])
    anywhere = pl.BlockSpec(memory_space=pl.ANY)
    table = pl.pallas_call(
        table_kernel,
        out_shape=jax.ShapeDtypeStruct((ROWS, SHARD), f32),
        in_specs=[anywhere] * 3,
        out_specs=FULL,
        scratch_shapes=[
            pltpu.VMEM((12, SHARD), f32),
            pltpu.VMEM((1, SHARD), f32),
            pltpu.VMEM((1, SHARD), jnp.int32),
            pltpu.SemaphoreType.DMA((3,)),
        ],
        compiler_params=PARAMS,
        cost_estimate=LONG,
        name="table",
    )(star_state, star_mass.reshape(1, SHARD), star_level.reshape(1, SHARD))
    tables = lax.all_gather(table, "core")
    sent = pl.pallas_call(
        lookup_kernel,
        out_shape=jax.ShapeDtypeStruct((SENDERS, 8, PART), f32),
        in_specs=[SCALARS] + [FULL] * 3,
        out_specs=FULL,
        compiler_params=PARAMS,
        name="lookup",
    )(where, slots, passed, tables)
    alone = exchange_groups(ALONE, [(x,) for x in range(4)])
    received = lax.all_to_all(sent, AXES, 0, 0, axis_index_groups=alone)
    partial = pl.pallas_call(
        force_kernel,
        out_shape=jax.ShapeDtypeStruct((MEMBERS, 8, PART), f32),
        in_specs=[FULL] * 2,
        out_specs=FULL,
        scratch_shapes=[pltpu.VMEM((32, PART), f32)],
        compiler_params=PARAMS,
        name="forces",
    )(received, tables)
    paired = exchange_groups(PAIRED, [(x, 3 - x) for x in range(2)])
    shares = lax.all_to_all(partial, AXES, 0, 0, axis_index_groups=paired)
    half_result = pl.pallas_call(
        correct_kernel,
        out_shape=jax.ShapeDtypeStruct((12, HALF), f32),
        in_specs=[FULL],
        out_specs=FULL,
        compiler_params=PARAMS,
        name="corrector",
    )(shares)
    halves = lax.all_gather(half_result, "core")
    result = jnp.concatenate([halves[0], halves[1]], 1)
    return jnp.where((active_slots >= 0)[None, :], result, 0.0)


def solution(mesh):
    split_mesh = Mesh(mesh.devices.reshape(SIZES), AXES)
    return jax.shard_map(
        local,
        mesh=split_mesh,
        in_specs=(P(None, BLK), P(BLK), P(BLK), P(ACT)),
        out_specs=P(None, ACT),
        check_vma=False,
    )
```
